512 devices in a mesh: gx: 4 (over z_lo), gy: 16 (over x, z_hi), gz: 8 (over y, core).
Axes of the slice: x: 4, y: 4, z: 16 (z_hi: 4, z_lo: 4; z = z_hi * 4 + z_lo), core: 2. Of those that a mesh axis runs over, the one named last changes fastest.
Arguments:
- e_field: float32 [3, 32, 128, 2048], P(None, 'gz', 'gx', 'gy'), may hold values from -6 to 6
- h_field: float32 [3, 32, 128, 2048], P(None, 'gz', 'gx', 'gy'), may hold values from -6 to 6
- pole_current: float32 [3, 32, 128, 2048], P(None, 'gz', 'gx', 'gy'), may hold values from -6 to 6
- material: int32 [32, 128, 2048], P('gz', 'gx', 'gy'), may hold values from 0 to 3
- pole_table: float32 [3, 4], replicated, may hold values from 0.2 to 0.9
- cotangent: float32 [16, 8, 4096], P(None, None, ('gx', 'gy', 'gz')), may hold values from -6 to 6
- cosines: float32 [2, 4096], P(None, ('gx', 'gy', 'gz')), may hold values from -0.7 to 0.7
- wavenumber: float32 [16], replicated, may hold values from 0.6 to 0.8
- time_phase: float32 [16], replicated, may hold values from -3.140625 to 3.140625
Outputs:
- e_next: float32 [3, 32, 128, 2048], P(None, 'gz', 'gx', 'gy')
- h_next: float32 [3, 32, 128, 2048], P(None, 'gz', 'gx', 'gy')
- pole_next: float32 [3, 32, 128, 2048], P(None, 'gz', 'gx', 'gy')
The draws below stay inside these ranges and needn't reach their ends.
All inputs are finite; a program needn't handle non-finite values.
Results may differ from the reference program's by a relative error of at most 0.0003.
Values sent between devices are 32-bit elements; how exact they have to be, the bound alone decides.
A program may use at most 64 MiB of HBM per device.

```python
import math
import jax
import jax.numpy as jnp
from jax import lax

FREQS = 16
DIRS = 4096
NPOLE = 4
NX = 128
NY = 2048
NZ = 32


def draw_cosines(key, part):
    sign_key = jax.random.fold_in(key, 11)
    size_key = jax.random.fold_in(key, 23)
    magnitude = jax.random.uniform(size_key, (2, DIRS), jnp.float32, 0.55, 0.7)
    positive = jax.random.bernoulli(sign_key, 0.5, (2, DIRS))
    signs = jnp.where(positive, 1.0, -1.0).astype(jnp.float32)
    return (signs * magnitude).astype(jnp.float32)


def plant(entries, rng, smallest, high):
    longest = entries.shape.index(max(entries.shape))
    spots = []
    for shift in (0, 1):
        where = [jax.random.randint(jax.random.fold_in(rng, axis), (), 0, length) for axis, length in enumerate(entries.shape)]
        where[longest] = (where[longest] + shift) % entries.shape[longest]
        spots.append(tuple(where))
    return entries.at[spots[0]].set(smallest).at[spots[1]].set(high)


def levels(own_key, shape, cuts, smallest, high):
    def one(axis_at, parts):
        steps = jax.random.uniform(jax.random.fold_in(jax.random.fold_in(own_key, 6), axis_at), (parts,), jnp.float32, smallest / len(cuts), high / len(cuts))
        return jnp.repeat(jnp.exp(steps), shape[axis_at] // parts).reshape((-1,) + (1,) * (len(shape) - axis_at - 1))

    loudness = one(*cuts[0])
    for cut in cuts[1:]:
        loudness = loudness * one(*cut)
    return loudness


def bell_draw(stream_key, extent, deviation, reach, cuts=(), kind=jnp.bfloat16):
    factor_of = levels(stream_key, extent, cuts, -0.22, 0.18) if cuts else 1.0
    array = jax.random.normal(stream_key, extent, jnp.float32) * deviation * factor_of
    return jnp.minimum(jnp.maximum(array, -reach), reach).astype(kind)


def setup_inputs(seed: int = 0) -> dict:
    splits = jax.random.split(jax.random.key(seed), 10)
    return {
        "e_field": bell_draw(splits[0], (3, NZ, NX, NY), 1.0, 6.0, ((1, 8), (2, 4), (3, 16)), jnp.float32),
        "h_field": bell_draw(splits[1], (3, NZ, NX, NY), 1.0, 6.0, ((1, 8), (2, 4), (3, 16)), jnp.float32),
        "pole_current": bell_draw(splits[2], (3, NZ, NX, NY), 1.0, 6.0, ((1, 8), (2, 4), (3, 16)), jnp.float32),
        "material": plant(jax.random.randint(splits[3], (NZ, NX, NY), 0, NPOLE), jax.random.fold_in(splits[3], 1), 0, NPOLE - 1).astype(jnp.int32),
        "pole_table": jnp.clip(jax.random.uniform(splits[4], (3, NPOLE), jnp.float32, 0.2, 0.9), 0.2, 0.9),
        "cotangent": bell_draw(splits[5], (FREQS, 8, DIRS), 1.0, 6.0, ((2, 512),), jnp.float32),
        "cosines": draw_cosines(jax.random.fold_in(splits[9], 71), 0),
        "wavenumber": jnp.clip(jnp.exp(jax.random.uniform(splits[7], (FREQS,), jnp.float32, math.log(0.6), math.log(0.8))), 0.6, 0.8),
        "time_phase": jnp.clip(jax.random.uniform(splits[8], (FREQS,), jnp.float32, -3.140625, 3.140625), -3.140625, 3.140625),
    }


courant = 0.5

def surface_source(cotangent, cosines, wavenumber, time_phase, xs, ys):
    count = cotangent.shape[2]
    rows_x = xs.shape[0]
    rows_y = ys.shape[0]

    def one_freq(total, freq):
        wave = wavenumber[freq]
        along_x = wave * cosines[0]
        along_y = wave * cosines[1]
        phase_x = xs[:, None] * along_x[None, :] - time_phase[freq]
        phase_y = ys[:, None] * along_y[None, :]
        cos_x = jnp.cos(phase_x)[None]
        sin_x = jnp.sin(phase_x)[None]
        weights = cotangent[freq]
        real_part = weights[0::2][:, None, :]
        imag_part = weights[1::2][:, None, :]
        first = real_part * cos_x - imag_part * sin_x
        second = -(real_part * sin_x + imag_part * cos_x)
        left = jnp.concatenate([first, second], axis=2).reshape(4 * rows_x, 2 * count)
        right = jnp.concatenate([jnp.cos(phase_y), jnp.sin(phase_y)], axis=1).T
        part = jnp.dot(left, right, preferred_element_type=jnp.float32, precision=lax.Precision.HIGHEST)
        return (total + part.reshape(4, rows_x, rows_y), None)
    start = jnp.zeros((4, rows_x, rows_y), jnp.float32)
    total, _ = lax.scan(one_freq, start, jnp.arange(cotangent.shape[0], dtype=jnp.int32))
    return total

def ahead(value, nearby, axis):
    rest = lax.slice_in_dim(value, 1, value.shape[axis], axis=axis)
    return jnp.concatenate([rest, nearby], axis) - value

def behind(value, nearby, axis):
    rest = lax.slice_in_dim(value, 0, value.shape[axis] - 1, axis=axis)
    return value - jnp.concatenate([nearby, rest], axis)

def edge_zero(value, axis):
    return jnp.zeros_like(lax.slice_in_dim(value, 0, 1, axis=axis))

def reference(e_field, h_field, pole_current, material, pole_table, cotangent, cosines, wavenumber, time_phase):
    xs = jnp.arange(NX).astype(jnp.float32)
    ys = jnp.arange(NY).astype(jnp.float32)
    source = surface_source(cotangent, cosines, wavenumber, time_phase, xs, ys) * (1.0 / math.sqrt(DIRS * FREQS))
    top = (jnp.arange(NZ) == NZ - 1).astype(jnp.float32)[:, None, None]
    ex, ey, ez = (e_field[0], e_field[1], e_field[2])
    curl_x = ahead(ez, edge_zero(ez, 2), 2) - ahead(ey, edge_zero(ey, 0), 0)
    curl_y = ahead(ex, edge_zero(ex, 0), 0) - ahead(ez, edge_zero(ez, 1), 1)
    curl_z = ahead(ey, edge_zero(ey, 1), 1) - ahead(ex, edge_zero(ex, 2), 2)
    hx = h_field[0] - courant * curl_x - courant * top * source[2][None]
    hy = h_field[1] - courant * curl_y - courant * top * source[3][None]
    hz = h_field[2] - courant * curl_z
    h_next = jnp.stack([hx, hy, hz])
    chosen = (material[None] == jnp.arange(NPOLE, dtype=jnp.int32)[:, None, None, None]).astype(jnp.float32)
    decay = lax.optimization_barrier(jnp.sum(chosen * pole_table[0][:, None, None, None], axis=0))
    drive = lax.optimization_barrier(jnp.sum(chosen * pole_table[1][:, None, None, None], axis=0))
    coef = lax.optimization_barrier(jnp.sum(chosen * pole_table[2][:, None, None, None], axis=0))
    pole_next = decay[None] * pole_current + drive[None] * e_field
    side_x = behind(hz, edge_zero(hz, 2), 2) - behind(hy, edge_zero(hy, 0), 0)
    side_y = behind(hx, edge_zero(hx, 0), 0) - behind(hz, edge_zero(hz, 1), 1)
    side_z = behind(hy, edge_zero(hy, 1), 1) - behind(hx, edge_zero(hx, 2), 2)
    curl_h = jnp.stack([side_x, side_y, side_z])
    inject = jnp.stack([top * source[0][None], top * source[1][None], jnp.zeros_like(ex)])
    e_next = e_field + coef[None] * (curl_h - 0.5 * (pole_next + pole_current)) - coef[None] * inject
    return (e_next, h_next, pole_next)
```

```python
import functools
import math

import jax
import jax.numpy as jnp
from jax import lax
from jax.experimental import pallas as pl
from jax.experimental.pallas import tpu as pltpu
from jax.sharding import PartitionSpec as P

PLANES = 4
COURANT = 0.5
MESH = pl.DeviceIdType.MESH
F32 = jnp.float32
BF16 = jnp.bfloat16

TURN = 2.0 * math.pi
TURN_HI = 6.28125
TURN_LO = TURN - TURN_HI


def sincos(phase):
    turns = jnp.floor(phase * (1.0 / TURN) + 0.5)
    rest = ((phase - turns * TURN_HI) - turns * TURN_LO) * 0.25
    sq = rest * rest
    sin = rest + rest * sq * (
        -1.6666654611e-1 + sq * (8.3321608736e-3 + sq * -1.9515295891e-4)
    )
    cos = 1.0 - 0.5 * sq + sq * sq * (
        4.166664568298827e-2 + sq * (-1.388731625493765e-3 + sq * 2.443315711809948e-5)
    )
    for _ in range(2):
        sin, cos = 2.0 * sin * cos, 1.0 - 2.0 * sin * sin
    return sin, cos


def times(a, b):
    return a[0] * b[0] - a[1] * b[1], a[0] * b[1] + a[1] * b[0]


def split(value):
    high = value.astype(BF16)
    return high, (value - high.astype(F32)).astype(BF16)


def iota(shape, dim):
    return lax.broadcasted_iota(jnp.int32, shape, dim)


def kernel(
    sizes, cot_in, cosines_in, wave_in, phase_in, table_in, e_in, h_in, p_in, m_in,
    e_out, h_out, p_out, cot, cosines, wave, phase, table, e_buf, h_buf, p_buf, m_buf, gat, xs, pq, yt, lt, part, total, from_x, from_gz, chunk, top_in,
    bound_x, bound_y, low, hx_out, hx_in, hy_out, hy_in, hz_in, kx_out, kx_in, ky_out, ky_in, kz_in,
    load_sem, gat_send, gat_recv, x_send, x_recv, gz_send, gz_recv, top_send, top_recv,
    bx_send, bx_recv, by_send, by_recv, halo_send, halo_recv,
):
    n_lo, n_hi, n_x, n_gz = sizes
    n_z = n_lo * n_hi
    depth, width_x, width_y = m_buf.shape
    half = width_x // 2
    gx, gy, gz = lax.axis_index("gx"), lax.axis_index("gy"), lax.axis_index("gz")
    z_hi = lax.rem(gy, n_hi)
    x = lax.div(gy, n_hi)
    core = lax.rem(gz, 2)
    z = z_hi * n_lo + gx
    is_top = gz == n_gz - 1

    def at(dx=0, dz=None, hi=None):
        if hi is not None:
            return {"gy": x * n_hi + lax.rem(z_hi + hi, n_hi)}
        if dz is not None:
            other = lax.rem(z + dz, n_z)
            return {"gx": lax.rem(other, n_lo), "gy": x * n_hi + lax.div(other, n_lo)}
        return {"gy": lax.rem(x + dx, n_x) * n_hi + z_hi}

    def step(axis, by):
        size = lax.axis_size(axis)
        return lax.rem(lax.axis_index(axis) + by + size, size)

    loads = [
        pltpu.make_async_copy(a, b, load_sem.at[i])
        for i, (a, b) in enumerate(
            (
                (cot_in, cot),
                (cosines_in, cosines),
                (wave_in, wave),
                (phase_in, phase),
                (e_in, e_buf),
                (h_in, h_buf),
                (p_in, p_buf),
                (m_in, m_buf),
                (table_in, table),
            )
        )
    ]
    for load in loads:
        load.start()

    if n_lo == 4:
        ring = [1, 2 + (n_z - 4) * core, n_z - 1]
    else:
        ring = [1]
    rows = n_gz and (2 * 4 * half) // n_gz

    def owner(kind, comp):
        return ((kind * 4 + comp) * half) // rows

    barrier = pltpu.get_barrier_semaphore()

    def greet(device):
        pl.semaphore_signal(barrier, inc=1, device_id=device, device_id_type=MESH)

    for k in range(1, n_hi):
        greet(at(hi=n_hi - k))
    for off in ring:
        greet(at(dz=n_z - off))
    for k in range(1, n_x):
        greet(at(dx=n_x - k))
    for k in range(1, n_gz):
        greet({"gz": step("gz", k)})
    for axis in ("gx", "gy"):
        for by in (1, -1):
            greet({axis: step(axis, by)})

    @pl.when(is_top)
    def _():
        for kind in range(2):
            greet({"gx": step("gx", -1), "gz": owner(kind, 3)})
            greet({"gy": step("gy", -1), "gz": owner(kind, 2)})

    extra = sum((gz == owner(kind, c)).astype(jnp.int32) for kind in range(2) for c in (2, 3))
    greeted = (n_hi - 1) + len(ring) + (n_x - 1) + (n_gz - 1) + 4

    for load in loads[:4]:
        load.wait()
    lane8 = iota((8, 128), 1)
    lane1 = iota((1, 128), 1)
    freq = lane1 % 16
    direction = lane1 // 16
    waves = jnp.zeros((1, 128), F32)
    times_ = jnp.zeros((1, 128), F32)
    cos_x = jnp.zeros((1, 128), F32)
    cos_y = jnp.zeros((1, 128), F32)
    for f in range(16):
        waves = jnp.where(freq == f, wave[f], waves)
        times_ = jnp.where(freq == f, phase[f], times_)
    for d in range(8):
        cos_x = jnp.where(direction == d, cosines[0, d], cos_x)
        cos_y = jnp.where(direction == d, cosines[1, d], cos_y)
    weights = jnp.concatenate([cot[:, d, :] for d in range(8)], axis=1)
    scale = 1.0 / math.sqrt(16.0 * 8 * n_lo * n_hi * n_x * n_gz)
    sin_t, cos_t = sincos(-times_)
    re = [weights[2 * c : 2 * c + 1] * scale for c in range(4)]
    im = [weights[2 * c + 1 : 2 * c + 2] * scale for c in range(4)]
    mine = gat.at[gx, z_hi]
    for c in range(4):
        mine[c : c + 1, :] = re[c] * cos_t - im[c] * sin_t
        mine[4 + c : 5 + c, :] = re[c] * sin_t + im[c] * cos_t
    mine[8:9, :] = waves * cos_x
    mine[9:10, :] = waves * cos_y

    pl.semaphore_wait(barrier, greeted + extra)

    def send(src, dst, send_sem, recv_sem, device):
        copy = pltpu.make_async_remote_copy(
            src_ref=src, dst_ref=dst, send_sem=send_sem, recv_sem=recv_sem,
            device_id=device, device_id_type=MESH,
        )
        return copy

    first = []
    for k in range(1, n_hi):
        block = gat.at[gx, z_hi, 0:10]
        copy = send(block, block, gat_send.at[k - 1], gat_recv.at[k - 1], at(hi=k))
        copy.start()
        first.append(copy)

    loads[4].wait()
    for i in range(2):
        for j in range(depth):
            hx_out[i * depth + j : i * depth + j + 1, :] = e_buf[1 + i, j, 0:1, :]
    packed = jnp.zeros((8, 128), F32)
    for i in range(2):
        for j in range(depth):
            for g in range(width_x // 8):
                to = (i * depth + j) * (width_x // 8) + g
                col = e_buf[2 * i, j, 8 * g : 8 * g + 8, :]
                packed = jnp.where(lane8 == to, pltpu.roll(col, to, 1) if to else col, packed)
    hy_out[...] = packed
    halo = [
        send(hx_out, hx_in, halo_send.at[0], halo_recv.at[0], {"gx": step("gx", -1)}),
        send(hy_out, hy_in, halo_send.at[1], halo_recv.at[1], {"gy": step("gy", -1)}),
        send(e_buf.at[0:2, 0], hz_in, halo_send.at[2], halo_recv.at[2], {"gz": step("gz", -1)}),
    ]
    for copy in halo:
        copy.start()

    for copy in first:
        copy.wait_recv()
    second = []
    for k, off in enumerate(ring):
        block = gat.at[gx, :, 0:10]
        copy = send(block, block, gat_send.at[3 + k], gat_recv.at[3 + k], at(dz=off))
        copy.start()
        second.append(copy)

    loads[5].wait()
    for copy in halo:
        copy.wait_recv()
    row = iota((width_x, 128), 0)
    lane = iota((width_x, 128), 1)
    keep_x = (gx < lax.axis_size("gx") - 1).astype(F32)
    keep_y = (gy < lax.axis_size("gy") - 1).astype(F32)
    keep_z = (gz < n_gz - 1).astype(F32)
    groups = width_x // 8

    def column(packed, which, lane_to):
        cols = []
        for g in range(groups):
            at_lane = which * groups + g
            by = (lane_to - at_lane) % 128
            cols.append(pltpu.roll(packed, by, 1) if by else packed)
        return jnp.concatenate(cols, axis=0)

    y_packed = hy_in[...] * keep_y
    for j in range(depth):
        ex, ey, ez = e_buf[0, j], e_buf[1, j], e_buf[2, j]
        if j < depth - 1:
            ex_z, ey_z = e_buf[0, j + 1], e_buf[1, j + 1]
        else:
            ex_z, ey_z = hz_in[0] * keep_z, hz_in[1] * keep_z

        def up_x(v, i):
            edge = hx_in[i * depth + j : i * depth + j + 1, :] * keep_x
            return jnp.where(row == width_x - 1, edge, pltpu.roll(v, width_x - 1, 0)) - v

        def up_y(v, i):
            edge = column(y_packed, i * depth + j, 127)
            return jnp.where(lane == 127, edge, pltpu.roll(v, 127, 1)) - v

        curl_x = up_y(ez, 1) - (ey_z - ey)
        curl_y = (ex_z - ex) - up_x(ez, 1)
        curl_z = up_x(ey, 0) - up_y(ex, 0)
        h_buf[0, j] = h_buf[0, j] - COURANT * curl_x
        h_buf[1, j] = h_buf[1, j] - COURANT * curl_y
        h_buf[2, j] = h_buf[2, j] - COURANT * curl_z

    for i in range(2):
        for j in range(depth):
            kx_out[i * depth + j : i * depth + j + 1, :] = h_buf[
                1 + i, j, width_x - 1 : width_x, :
            ]
    packed = jnp.zeros((8, 128), F32)
    for i in range(2):
        for j in range(depth):
            for g in range(groups):
                to = (i * depth + j) * groups + g
                col = h_buf[2 * i, j, 8 * g : 8 * g + 8, :]
                packed = jnp.where(lane8 == to, pltpu.roll(col, to + 1, 1), packed)
    ky_out[...] = packed
    halo2 = [
        send(kx_out, kx_in, halo_send.at[3], halo_recv.at[3], {"gx": step("gx", 1)}),
        send(ky_out, ky_in, halo_send.at[4], halo_recv.at[4], {"gy": step("gy", 1)}),
        send(
            h_buf.at[0:2, depth - 1], kz_in, halo_send.at[5], halo_recv.at[5],
            {"gz": step("gz", 1)},
        ),
    ]
    for copy in halo2:
        copy.start()

    for copy in second:
        copy.wait_recv()
    row8 = iota((8, 128), 0)
    rowf = row8.astype(F32)
    centre = (gx * width_x).astype(F32) + (0.5 * width_x - 0.5)
    tile_y = ((row8 * n_hi + z_hi) * width_y).astype(F32)
    mul_x = jnp.where(row8 < 4, centre, jnp.where(row8 == 7, 8.0, 0.0))
    mul_y = jnp.where(
        row8 < 4,
        tile_y,
        jnp.where(row8 == 4, 8.0, jnp.where(row8 == 5, 32.0, jnp.where(row8 == 6, 64.0, 0.0))),
    )
    sign = jnp.where(row8 < 4, -1.0, 1.0)

    def factors(s, carry):
        lo = lax.div(s, n_hi)
        hi = lax.rem(s, n_hi)
        along_x = gat[lo, hi, 8:9, :]
        along_y = gat[lo, hi, 9:10, :]
        w = gat[lo, hi, 0:8, :]
        turned = pltpu.roll(w, 4, 0) * sign
        sin_m, cos_m = sincos(along_x * mul_x + along_y * mul_y)
        for t in range(n_x):
            pq[t, s] = w * cos_m[t : t + 1] + turned * sin_m[t : t + 1]
        sin_b, cos_b = sincos(along_x * (rowf + 0.5))
        more = times((cos_b, sin_b), (cos_m[7:8], sin_m[7:8]))
        xs[s, 0, 0:8] = cos_b
        xs[s, 0, 8:16] = more[0]
        xs[s, 1, 0:8] = sin_b
        xs[s, 1, 8:16] = more[1]
        sin_b, cos_b = sincos(along_y * rowf)
        e8 = (cos_m[4:5], sin_m[4:5])
        more = times((cos_b, sin_b), e8)
        block = (jnp.concatenate([cos_b, more[0]], 0), jnp.concatenate([sin_b, more[1]], 0))
        blocks = [block]
        for power in (times(e8, e8), (cos_m[5:6], sin_m[5:6]), (cos_m[6:7], sin_m[6:7])):
            blocks = blocks + [times(b, power) for b in blocks]
        for g, b in enumerate(blocks):
            for kind in range(2):
                high, lowp = split(b[kind])
                base = pl.multiple_of(s * 256 + kind * 128, 128)
                yt[16 * g : 16 * g + 16, pl.ds(base, 128)] = high
                yt[128 + 16 * g : 144 + 16 * g, pl.ds(base, 128)] = lowp
        return carry

    lax.fori_loop(0, n_z, factors, 0)

    def tile(t):
        def build(s, carry):
            cx, sx = xs[s, 0], xs[s, 1]
            nx = -sx
            for c in range(4):
                p = pq[t, s, c : c + 1, :]
                nq = -pq[t, s, 4 + c : 5 + c, :]
                products = ((p * cx, nq * cx), (nq * sx, p * nx))
                for kind in range(2):
                    r = (kind * 4 + c) * half
                    for k in range(2):
                        high, lowp = split(products[kind][k])
                        base = pl.multiple_of(s * 256 + k * 128, 128)
                        lt[r : r + half, pl.ds(base, 128)] = high
                        lt[128 + r : 128 + r + half, pl.ds(base, 128)] = lowp
            return carry

        lax.fori_loop(0, n_z, build, 0)
        both = lax.dot_general(
            lt[...], yt[...], (((1,), (1,)), ((), ())), preferred_element_type=F32
        )
        return both[0:128, 0:128] + (both[0:128, 128:256] + both[128:256, 0:128])

    def to_x(k):
        return send(
            part.at[k - 1], from_x.at[k - 1], x_send.at[k - 1], x_recv.at[k - 1],
            {"gy": lax.rem(x + k, n_x) * n_hi + z_hi},
        )

    def other(k, carry):
        part[k - 1] = tile(lax.rem(x + k, n_x))
        to_x(k).start()
        return carry

    lax.fori_loop(1, n_x, other, 0)
    own = tile(x)

    for k in range(1, n_x):
        to_x(k).wait_recv()
        own = own + from_x[k - 1]
    total[...] = own

    spread = []
    for k in range(1, n_gz):
        to = step("gz", k)
        copy = send(
            total.at[pl.ds(pl.multiple_of(to * rows, rows), rows)], from_gz.at[k - 1],
            gz_send.at[k - 1], gz_recv.at[k - 1], {"gz": to},
        )
        copy.start()
        spread.append(copy)

    for load in loads[6:]:
        load.wait()
    for copy in halo2:
        copy.wait_recv()
    keep_x = (gx > 0).astype(F32)
    keep_y = (gy > 0).astype(F32)
    keep_z = (gz > 0).astype(F32)
    y_packed = ky_in[...] * keep_y

    def chosen(which, m):
        value = jnp.full(m.shape, table[which, 3], F32)
        for i in range(3):
            value = jnp.where(m == i, table[which, i], value)
        return value

    for j in range(depth):
        hx, hy, hz = h_buf[0, j], h_buf[1, j], h_buf[2, j]
        if j > 0:
            hx_z, hy_z = h_buf[0, j - 1], h_buf[1, j - 1]
        else:
            hx_z, hy_z = kz_in[0] * keep_z, kz_in[1] * keep_z

        def down_x(v, i):
            edge = kx_in[i * depth + j : i * depth + j + 1, :] * keep_x
            return v - jnp.where(row == 0, edge, pltpu.roll(v, 1, 0))

        def down_y(v, i):
            edge = column(y_packed, i * depth + j, 0)
            return v - jnp.where(lane == 0, edge, pltpu.roll(v, 1, 1))

        side = (
            down_y(hz, 1) - (hy - hy_z),
            (hx - hx_z) - down_x(hz, 1),
            down_x(hy, 0) - down_y(hx, 0),
        )
        m = m_buf[j]
        decay, drive, coef = chosen(0, m), chosen(1, m), chosen(2, m)
        for i in range(3):
            e, pole = e_buf[i, j], p_buf[i, j]
            after = decay * pole + drive * e
            p_out[i, j] = after
            e_out[i, j] = e + coef * (side[i] - 0.5 * (after + pole))
            h_out[i, j] = h_buf[i, j]

    summed = total[pl.ds(pl.multiple_of(gz * rows, rows), rows), :]
    for copy in spread:
        copy.wait_recv()
    for k in range(n_gz - 1):
        summed = summed + from_gz[k]
    chunk[...] = summed

    def to_top():
        return send(
            chunk, top_in.at[pl.ds(pl.multiple_of(gz * rows, rows), rows)], top_send.at[0],
            top_recv.at[gz], {"gz": n_gz - 1},
        )

    @pl.when(jnp.logical_not(is_top))
    def _():
        to_top().start()

    def edge_x(kind):
        r = ((kind * 4 + 3) * half) % rows + half - 8
        return send(
            chunk.at[r : r + 8], bound_x.at[kind], bx_send.at[kind], bx_recv.at[kind],
            {"gx": step("gx", 1), "gz": n_gz - 1},
        )

    def edge_y(kind):
        r = ((kind * 4 + 2) * half) % rows
        return send(
            chunk.at[r : r + half], bound_y.at[kind], by_send.at[kind], by_recv.at[kind],
            {"gy": step("gy", 1), "gz": n_gz - 1},
        )

    for kind in range(2):
        @pl.when(gz == owner(kind, 3))
        def _():
            edge_x(kind).start()

        @pl.when(gz == owner(kind, 2))
        def _():
            edge_y(kind).start()

    @pl.when(is_top)
    def _():
        top_in[(n_gz - 1) * rows : n_gz * rows] = chunk[...]
        for k in range(n_gz - 1):
            send(
                chunk, top_in.at[k * rows : (k + 1) * rows], top_send.at[0], top_recv.at[k],
                {"gz": 0},
            ).wait_recv()
        for kind in range(2):
            edge_x(kind).wait_recv()
            edge_y(kind).wait_recv()

        def unfold(even, odd, at_row):
            lower = even - odd
            for j in range(half):
                low[at_row, half - 1 - j : half - j, :] = lower[j : j + 1, :]
            return jnp.concatenate([low[at_row], even + odd], axis=0)

        src = [
            unfold(
                top_in[c * half : (c + 1) * half, :],
                top_in[(4 + c) * half : (5 + c) * half, :],
                c,
            )
            for c in range(4)
        ]
        near_y = unfold(bound_y[0], bound_y[1], 4) * keep_y
        near_x = (bound_x[0, 7:8, :] + bound_x[1, 7:8, :]) * keep_x
        last = depth - 1
        coef = chosen(2, m_buf[last])
        h_out[0, last] = h_out[0, last] - COURANT * src[2]
        h_out[1, last] = h_out[1, last] - COURANT * src[3]
        behind_x = src[3] - jnp.where(row == 0, near_x, pltpu.roll(src[3], 1, 0))
        behind_y = src[2] - jnp.where(lane == 0, pltpu.roll(near_y, 1, 1), pltpu.roll(src[2], 1, 1))
        e_out[0, last] = e_out[0, last] + coef * (COURANT * src[3] - src[0])
        e_out[1, last] = e_out[1, last] - coef * (COURANT * src[2] + src[1])
        e_out[2, last] = e_out[2, last] - coef * (COURANT * (behind_x - behind_y))

    for copy in first + second + halo + halo2 + spread:
        copy.wait_send()
    for k in range(1, n_x):
        to_x(k).wait_send()

    @pl.when(jnp.logical_not(is_top))
    def _():
        to_top().wait_send()

    for kind in range(2):
        @pl.when(gz == owner(kind, 3))
        def _():
            edge_x(kind).wait_send()

        @pl.when(gz == owner(kind, 2))
        def _():
            edge_y(kind).wait_send()


def local(
    sizes, e_field, h_field, pole_current, material, pole_table, cotangent, cosines, wavenumber,
    time_phase,
):
    n_lo, n_hi, n_x, n_gz = sizes
    n_z = n_lo * n_hi
    depth, width_x, width_y = material.shape
    half = width_x // 2
    rows = 8 * half // n_gz
    block = (3, depth, width_x, width_y)
    vmem = pl.BlockSpec(memory_space=pltpu.VMEM)
    hbm = pl.BlockSpec(memory_space=pl.ANY)
    dma = pltpu.SemaphoreType.DMA
    cot = jnp.transpose(cotangent, (1, 2, 0))
    field = jax.ShapeDtypeStruct(block, F32)
    return tuple(
        pl.pallas_call(
            functools.partial(kernel, sizes),
            out_shape=(field, field, field),
            in_specs=[hbm] * 9,
            out_specs=(vmem, vmem, vmem),
            scratch_shapes=[
                pltpu.VMEM((8, 8, 16), F32),
                pltpu.SMEM((2, 8), F32),
                pltpu.SMEM((16,), F32),
                pltpu.SMEM((16,), F32),
                pltpu.SMEM((3, 4), F32),
                pltpu.VMEM(block, F32),
                pltpu.VMEM(block, F32),
                pltpu.VMEM(block, F32),
                pltpu.VMEM((depth, width_x, width_y), jnp.int32),
                pltpu.VMEM((n_lo, n_hi, 16, 128), F32),
                pltpu.VMEM((n_z, 2, half, 128), F32),
                pltpu.VMEM((n_x, n_z, 8, 128), F32),
                pltpu.VMEM((256, n_z * 256), BF16),
                pltpu.VMEM((256, n_z * 256), BF16),
                pltpu.VMEM((n_x - 1, 128, 128), F32),
                pltpu.VMEM((128, 128), F32),
                pltpu.VMEM((n_x - 1, 128, 128), F32),
                pltpu.VMEM((n_gz - 1, rows, 128), F32),
                pltpu.VMEM((rows, 128), F32),
                pltpu.VMEM((128, 128), F32),
                pltpu.VMEM((2, 8, 128), F32),
                pltpu.VMEM((2, half, 128), F32),
                pltpu.VMEM((5, half, 128), F32),
                pltpu.VMEM((8, 128), F32),
                pltpu.VMEM((8, 128), F32),
                pltpu.VMEM((8, 128), F32),
                pltpu.VMEM((8, 128), F32),
                pltpu.VMEM((2, width_x, 128), F32),
                pltpu.VMEM((8, 128), F32),
                pltpu.VMEM((8, 128), F32),
                pltpu.VMEM((8, 128), F32),
                pltpu.VMEM((8, 128), F32),
                pltpu.VMEM((2, width_x, 128), F32),
                dma((9,)),
                dma((6,)),
                dma((6,)),
                dma((n_x - 1,)),
                dma((n_x - 1,)),
                dma((n_gz - 1,)),
                dma((n_gz - 1,)),
                dma((1,)),
                dma((n_gz,)),
                dma((2,)),
                dma((2,)),
                dma((2,)),
                dma((2,)),
                dma((6,)),
                dma((6,)),
            ],
            compiler_params=pltpu.CompilerParams(
                collective_id=0, has_side_effects=True, vmem_limit_bytes=60 * 1024 * 1024
            ),
        )(cot, cosines, wavenumber, time_phase, pole_table, e_field, h_field, pole_current, material)
    )


def solution(mesh):
    sizes = (mesh.shape["gx"], PLANES, mesh.shape["gy"] // PLANES, mesh.shape["gz"])
    field = P(None, "gz", "gx", "gy")
    in_specs = (
        field,
        field,
        field,
        P("gz", "gx", "gy"),
        P(),
        P(None, None, ("gx", "gy", "gz")),
        P(None, ("gx", "gy", "gz")),
        P(),
        P(),
    )
    return jax.shard_map(
        functools.partial(local, sizes),
        mesh=mesh,
        in_specs=in_specs,
        out_specs=(field, field, field),
        check_vma=False,
    )
```

```python
import functools
import math

import jax
import jax.numpy as jnp
from jax import lax
from jax.experimental import pallas as pl
from jax.experimental.pallas import tpu as pltpu
from jax.sharding import PartitionSpec as P

PLANES = 4
COURANT = 0.5
MESH = pl.DeviceIdType.MESH
F32 = jnp.float32
BF16 = jnp.bfloat16

TURN = 2.0 * math.pi
TURN_HI = 6.28125
TURN_LO = TURN - TURN_HI


def sincos(phase):
    turns = jnp.floor(phase * (1.0 / TURN) + 0.5)
    rest = ((phase - turns * TURN_HI) - turns * TURN_LO) * 0.25
    sq = rest * rest
    sin = rest + rest * sq * (
        -1.6666654611e-1 + sq * (8.3321608736e-3 + sq * -1.9515295891e-4)
    )
    cos = 1.0 - 0.5 * sq + sq * sq * (
        4.166664568298827e-2 + sq * (-1.388731625493765e-3 + sq * 2.443315711809948e-5)
    )
    for _ in range(2):
        sin, cos = 2.0 * sin * cos, 1.0 - 2.0 * sin * sin
    return sin, cos


def times(a, b):
    return a[0] * b[0] - a[1] * b[1], a[0] * b[1] + a[1] * b[0]


def split(value):
    high = value.astype(BF16)
    return high, (value - high.astype(F32)).astype(BF16)


def iota(shape, dim):
    return lax.broadcasted_iota(jnp.int32, shape, dim)


def kernel(
    sizes, cot_in, cosines_in, wave_in, phase_in, table_in, e_in, h_in, p_in, m_in,
    e_out, h_out, p_out, cot, cosines, wave, phase, table, e_buf, h_buf, p_buf, m_buf,
    gat, xs, edge, pq, yt, lt, acc, from_x, total, from_gz, low,
    hx_out, hx_in, hy_out, hy_in, hz_in, kx_out, kx_in, ky_out, ky_in, kz_in,
    load_sem, gat_send, gat_recv, x_send, x_recv, gz_send, gz_recv, halo_send, halo_recv,
):
    n_lo, n_hi, n_x, n_gz = sizes
    n_z = n_lo * n_hi
    n_half = n_z // 2
    depth, width_x, width_y = m_buf.shape
    half = width_x // 2
    gx, gy, gz = lax.axis_index("gx"), lax.axis_index("gy"), lax.axis_index("gz")
    z_hi = gy & (n_hi - 1)
    x = gy // n_hi
    z = z_hi * n_lo + gx
    is_top = gz == n_gz - 1

    def plane(other):
        return {"gx": other & (n_lo - 1), "gy": x * n_hi + other // n_lo}

    def column_of(k):
        return {"gy": ((x + k) & (n_x - 1)) * n_hi + z_hi}

    def copy_to(src, dst, send_sem, recv_sem, device):
        return pltpu.make_async_remote_copy(
            src_ref=src, dst_ref=dst, send_sem=send_sem, recv_sem=recv_sem,
            device_id=device, device_id_type=MESH,
        )

    loads = [
        pltpu.make_async_copy(a, b, load_sem.at[i])
        for i, (a, b) in enumerate(
            (
                (cot_in, cot),
                (cosines_in, cosines),
                (wave_in, wave),
                (phase_in, phase),
                (e_in, e_buf),
                (h_in, h_buf),
                (p_in, p_buf),
                (m_in, m_buf),
                (table_in, table),
            )
        )
    ]
    for load in loads:
        load.start()

    wrap_low = jnp.logical_and(z_hi == n_hi - 1, x < n_x - 1)
    wrap_high = jnp.logical_and(z_hi == 0, x > 0)

    barrier = pltpu.get_barrier_semaphore()

    def greet(device):
        pl.semaphore_signal(barrier, inc=1, device_id=device, device_id_type=MESH)

    def greet_plane(other, carry):
        greet(plane(other))
        return carry

    lax.fori_loop(z + 1, n_z, greet_plane, 0)
    for k in range(1, n_x):
        greet(column_of(k))

    @pl.when(gz < n_gz - 1)
    def _():
        greet({"gz": gz + 1})

    @pl.when(is_top)
    def _():
        for k in range(n_gz - 1):
            greet({"gz": k})

    @pl.when(wrap_high)
    def _():
        greet({"gy": gy - 1})

    greeted = (
        z
        + (n_x - 1)
        + (gz > 0).astype(jnp.int32)
        + (gz < n_gz - 1).astype(jnp.int32)
        + wrap_low.astype(jnp.int32)
    )

    for load in loads[:4]:
        load.wait()
    row8 = iota((8, 128), 0)
    lane8 = iota((8, 128), 1)
    lane1 = iota((1, 128), 1)
    freq = lane1 & 15
    direction = lane1 >> 4
    waves = jnp.zeros((1, 128), F32)
    delays = jnp.zeros((1, 128), F32)
    cos_x = jnp.zeros((1, 128), F32)
    cos_y = jnp.zeros((1, 128), F32)
    for f in range(16):
        waves = jnp.where(freq == f, wave[f], waves)
        delays = jnp.where(freq == f, phase[f], delays)
    for d in range(8):
        cos_x = jnp.where(direction == d, cosines[0, d], cos_x)
        cos_y = jnp.where(direction == d, cosines[1, d], cos_y)
    weights = jnp.concatenate([cot[:, d, :] for d in range(8)], axis=1)
    scale = 1.0 / math.sqrt(16.0 * 8 * n_lo * n_hi * n_x * n_gz)
    sin_t, cos_t = sincos(-delays)
    re = [weights[2 * c : 2 * c + 1] * scale for c in range(4)]
    im = [weights[2 * c + 1 : 2 * c + 2] * scale for c in range(4)]
    mine = gat.at[z]
    for c in range(4):
        mine[c : c + 1, :] = re[c] * cos_t - im[c] * sin_t
        mine[4 + c : 5 + c, :] = re[c] * sin_t + im[c] * cos_t
    mine[8:9, :] = waves * cos_x
    mine[9:10, :] = waves * cos_y

    pl.semaphore_wait(barrier, greeted)

    def share(other):
        block = gat.at[z, 0:10]
        return copy_to(block, block, gat_send.at[other], gat_recv.at[z], plane(other))

    def arrival(other):
        block = gat.at[other, 0:10]
        return copy_to(block, block, gat_send.at[other], gat_recv.at[other], plane(other))

    def share_down(other, carry):
        share(other).start()
        return carry

    lax.fori_loop(0, z, share_down, 0)

    loads[4].wait()
    groups = width_x // 8
    low_x, high_x = gx > 0, gx < n_lo - 1
    low_z, high_z = gz > 0, gz < n_gz - 1
    low_y, high_y = gy > 0, gy < n_hi * n_x - 1
    plain_low_y, plain_high_y = z_hi > 0, z_hi < n_hi - 1
    ex_copy = copy_to(hx_out, hx_in, halo_send.at[0], halo_recv.at[0], {"gx": gx - 1})
    ey_copy = copy_to(hy_out, hy_in, halo_send.at[1], halo_recv.at[1], {"gy": gy - 1})
    ez_copy = copy_to(
        e_buf.at[0:2, 0], hz_in, halo_send.at[2], halo_recv.at[2], {"gz": gz - 1}
    )
    hx_copy = copy_to(kx_out, kx_in, halo_send.at[3], halo_recv.at[3], {"gx": gx + 1})
    hy_copy = copy_to(ky_out, ky_in, halo_send.at[4], halo_recv.at[4], {"gy": gy + 1})
    hz_copy = copy_to(
        h_buf.at[0:2, depth - 1], kz_in, halo_send.at[5], halo_recv.at[5], {"gz": gz + 1}
    )

    def when(flag, action):
        @pl.when(flag)
        def _():
            action()

    when(low_z, ez_copy.start)
    for i in range(2):
        for j in range(depth):
            hx_out[i * depth + j : i * depth + j + 1, :] = e_buf[1 + i, j, 0:1, :]
    when(low_x, ex_copy.start)
    packed = jnp.zeros((8, 128), F32)
    for i in range(2):
        for j in range(depth):
            for g in range(groups):
                to = (i * depth + j) * groups + g
                col = e_buf[2 * i, j, 8 * g : 8 * g + 8, :]
                packed = jnp.where(lane8 == to, pltpu.roll(col, to, 1) if to else col, packed)
    hy_out[...] = packed
    when(plain_low_y, ey_copy.start)

    loads[5].wait()
    when(high_x, ex_copy.wait_recv)
    when(plain_high_y, ey_copy.wait_recv)
    when(high_z, ez_copy.wait_recv)
    row = iota((width_x, 128), 0)
    lane = iota((width_x, 128), 1)

    def column(packed, which, lane_to):
        cols = []
        for g in range(groups):
            by = (lane_to - which * groups - g) % 128
            cols.append(pltpu.roll(packed, by, 1) if by else packed)
        return jnp.concatenate(cols, axis=0)

    x_edges = jnp.where(high_x, hx_in[...], 0.0)
    y_packed = jnp.where(plain_high_y, hy_in[...], 0.0)
    z_edges = [jnp.where(high_z, hz_in[i], 0.0) for i in range(2)]
    for j in range(depth):
        ex, ey, ez = e_buf[0, j], e_buf[1, j], e_buf[2, j]
        ex_z, ey_z = (e_buf[0, j + 1], e_buf[1, j + 1]) if j < depth - 1 else z_edges

        def up_x(v, i):
            next_row = x_edges[i * depth + j : i * depth + j + 1, :]
            return jnp.where(row == width_x - 1, next_row, pltpu.roll(v, width_x - 1, 0)) - v

        def up_y(v, i):
            next_col = column(y_packed, i * depth + j, 127)
            return jnp.where(lane == 127, next_col, pltpu.roll(v, 127, 1)) - v

        h_buf[0, j] = h_buf[0, j] - COURANT * (up_y(ez, 1) - (ey_z - ey))
        h_buf[1, j] = h_buf[1, j] - COURANT * ((ex_z - ex) - up_x(ez, 1))
        h_buf[2, j] = h_buf[2, j] - COURANT * (up_x(ey, 0) - up_y(ex, 0))

    packed = jnp.zeros((8, 128), F32)
    for i in range(2):
        for j in range(depth):
            for g in range(groups):
                to = (i * depth + j) * groups + g
                col = h_buf[2 * i, j, 8 * g : 8 * g + 8, :]
                packed = jnp.where(lane8 == to, pltpu.roll(col, to + 1, 1), packed)
    ky_out[...] = packed
    when(high_y, hy_copy.start)

    def send_hx_hz():
        for i in range(2):
            for j in range(depth):
                kx_out[i * depth + j : i * depth + j + 1, :] = h_buf[
                    1 + i, j, width_x - 1 : width_x, :
                ]
        when(high_x, hx_copy.start)
        when(high_z, hz_copy.start)

    when(jnp.logical_not(wrap_low), send_hx_hz)

    def collect(first):
        def one(i, carry):
            other = first + i

            @pl.when(other != z)
            def _():
                arrival(other).wait_recv()

            @pl.when(other > z)
            def _():
                share(other).start()

            return carry

        lax.fori_loop(0, n_half, one, 0)

    rowf = row8.astype(F32)
    centre = (gx * width_x).astype(F32) + (0.5 * width_x - 0.5)
    tile_y = ((row8 * n_hi + z_hi) * width_y).astype(F32)
    mul_x = jnp.where(
        row8 < 4, centre, jnp.where(row8 == 5, half + 0.5, jnp.where(row8 == 7, 8.0, 0.0))
    )
    mul_y = jnp.where(
        row8 < 4, tile_y, jnp.where(row8 == 4, 8.0, jnp.where(row8 == 6, 64.0, 0.0))
    )
    sign = jnp.where(row8 < 4, -1.0, 1.0)

    def factors_of(first):
        def factors(s, carry):
            along_x = gat[first + s, 8:9, :]
            along_y = gat[first + s, 9:10, :]
            w = gat[first + s, 0:8, :]
            turned = pltpu.roll(w, 4, 0) * sign
            sin_m, cos_m = sincos(along_x * mul_x + along_y * mul_y)
            for t in range(n_x):
                pq[t, s] = w * cos_m[t : t + 1] + turned * sin_m[t : t + 1]
            sin_b, cos_b = sincos(along_x * (rowf + 0.5))
            more = times((cos_b, sin_b), (cos_m[7:8], sin_m[7:8]))
            xs[s, 0, 0:8] = cos_b
            xs[s, 0, 8:16] = more[0]
            xs[s, 1, 0:8] = sin_b
            xs[s, 1, 8:16] = more[1]
            edge[s, 0:1] = cos_m[5:6]
            edge[s, 1:2] = -sin_m[5:6]
            sin_b, cos_b = sincos(along_y * rowf)
            edge[s, 2:3] = cos_b[1:2]
            edge[s, 3:4] = -sin_b[1:2]
            e8 = (cos_m[4:5], sin_m[4:5])
            e16 = times(e8, e8)
            more = times((cos_b, sin_b), e8)
            block = (jnp.concatenate([cos_b, more[0]], 0), jnp.concatenate([sin_b, more[1]], 0))
            blocks = [block]
            for power in (e16, times(e16, e16), (cos_m[6:7], sin_m[6:7])):
                blocks = blocks + [times(b, power) for b in blocks]
            for g, b in enumerate(blocks):
                for kind in range(2):
                    high, lowp = split(b[kind])
                    base = pl.multiple_of(s * 256 + kind * 128, 128)
                    yt[16 * g : 16 * g + 16, pl.ds(base, 128)] = high
                    yt[128 + 16 * g : 144 + 16 * g, pl.ds(base, 128)] = lowp
            return carry

        lax.fori_loop(0, n_half, factors, 0)

    row16 = iota((16, 128), 0)
    lane16 = iota((16, 128), 1)

    def tile(t):
        def build(s, cols):
            cx, sx = xs[s, 0], xs[s, 1]
            nx = -sx

            def put(r, k, value):
                high, lowp = split(value)
                base = pl.multiple_of(s * 256 + k * 128, 128)
                lt[r : r + 16, pl.ds(base, 128)] = high
                lt[144 + r : 160 + r, pl.ds(base, 128)] = lowp

            for c in range(4):
                p = pq[t, s, c : c + 1, :]
                nq = -pq[t, s, 4 + c : 5 + c, :]
                products = ((p * cx, nq * cx), (nq * sx, p * nx))
                for kind in range(2):
                    for k in range(2):
                        put((kind * 4 + c) * half, k, products[kind][k])
                if c == 2:
                    cy, sy = edge[s, 2:3, :], edge[s, 3:4, :]
                    cols = tuple(
                        old + (new[0] * cy + new[1] * sy) for old, new in zip(cols, products)
                    )
                if c == 3:
                    ox, oy = edge[s, 0:1, :], edge[s, 1:2, :]
                    put(128, 0, jnp.broadcast_to(p * ox + nq * oy, (16, 128)))
                    put(128, 1, jnp.broadcast_to(nq * ox - p * oy, (16, 128)))
            return cols

        zero = jnp.zeros((16, 128), F32)
        cols = lax.fori_loop(0, n_half, build, (zero, zero))
        both = lax.dot_general(
            lt[...], yt[...], (((1,), (1,)), ((), ())), preferred_element_type=F32
        )
        main = both[0:136, 0:128] + (both[0:136, 128:256] + both[144:280, 0:128])
        before = jnp.zeros((1, 128), F32)
        for kind in range(2):
            sums = jnp.sum(cols[kind], axis=1, keepdims=True)
            placed = jnp.where(lane16 == row16 + 16 * kind, sums, 0.0)
            before = before + jnp.sum(placed, axis=0, keepdims=True)
        return main[0:128], jnp.where(row8 == 0, main[128:136], jnp.where(row8 == 1, before, 0.0))

    own_half = (z // n_half) * n_half
    other_half = n_half - own_half
    collect(own_half)
    factors_of(own_half)

    def first_pass(k, carry):
        main, rest = tile((x + k) & (n_x - 1))
        acc[k, 0:128] = main
        acc[k, 128:136] = rest
        return carry

    lax.fori_loop(0, n_x, first_pass, 0)
    collect(other_half)

    @pl.when(wrap_high)
    def _():
        hy_copy.wait_recv()
        ey_copy.start()

    factors_of(other_half)

    def to_x(k):
        return copy_to(
            acc.at[k], from_x.at[k - 1], x_send.at[k - 1], x_recv.at[k - 1], column_of(k)
        )

    def second_pass(i, carry):
        k = jnp.where(i == n_x - 1, 0, jnp.where(i == 0, n_x // 2, jnp.where(i == 1, 1, i + 1)))
        main, rest = tile((x + k) & (n_x - 1))
        acc[k, 0:128] = acc[k, 0:128] + main
        acc[k, 128:136] = acc[k, 128:136] + rest

        @pl.when(k > 0)
        def _():
            to_x(k).start()

        return carry

    lax.fori_loop(0, n_x, second_pass, 0)

    @pl.when(wrap_low)
    def _():
        ey_copy.wait_recv()
        late = hy_in[...]
        for j in range(depth):
            h_buf[0, j] = h_buf[0, j] - jnp.where(
                lane == 127, COURANT * column(late, depth + j, 127), 0.0
            )
            h_buf[2, j] = h_buf[2, j] + jnp.where(
                lane == 127, COURANT * column(late, j, 127), 0.0
            )
        send_hx_hz()

    for load in loads[6:]:
        load.wait()
    when(low_x, hx_copy.wait_recv)
    when(plain_low_y, hy_copy.wait_recv)
    when(low_z, hz_copy.wait_recv)
    x_edges = jnp.where(low_x, kx_in[...], 0.0)
    y_packed = jnp.where(low_y, ky_in[...], 0.0)
    z_edges = [jnp.where(low_z, kz_in[i], 0.0) for i in range(2)]
    missing = jnp.where(wrap_high, COURANT, 0.0)

    def chosen(which, m):
        value = jnp.full(m.shape, table[which, 3], F32)
        for i in range(3):
            value = jnp.where(m == i, table[which, i], value)
        return value

    for j in range(depth):
        hx, hy, hz = h_buf[0, j], h_buf[1, j], h_buf[2, j]
        hx_z, hy_z = (h_buf[0, j - 1], h_buf[1, j - 1]) if j > 0 else z_edges
        ex, ey, ez = e_buf[0, j], e_buf[1, j], e_buf[2, j]

        def down_x(v, i):
            last_row = x_edges[i * depth + j : i * depth + j + 1, :]
            return v - jnp.where(row == 0, last_row, pltpu.roll(v, 1, 0))

        def down_y(v, i, rest):
            last_col = column(y_packed, i * depth + j, 0) + rest
            return v - jnp.where(lane == 0, last_col, pltpu.roll(v, 1, 1))

        side = (
            down_y(hz, 1, missing * ex) - (hy - hy_z),
            (hx - hx_z) - down_x(hz, 1),
            down_x(hy, 0) - down_y(hx, 0, -missing * ez),
        )
        m = m_buf[j]
        decay, drive, coef = chosen(0, m), chosen(1, m), chosen(2, m)
        for i, e in enumerate((ex, ey, ez)):
            pole = p_buf[i, j]
            after = decay * pole + drive * e
            p_out[i, j] = after
            e_out[i, j] = e + coef * (side[i] - 0.5 * (after + pole))
            h_out[i, j] = h_buf[i, j]

    for k in range(1, n_x):
        to_x(k).wait_recv()
    total[...] = sum((from_x[k] for k in range(n_x - 1)), acc[0])

    def to_top(k):
        return copy_to(
            total, from_gz.at[k], gz_send.at[0], gz_recv.at[k], {"gz": n_gz - 1}
        )

    @pl.when(jnp.logical_not(is_top))
    def _():
        to_top(gz).start()

    @pl.when(is_top)
    def _():
        for k in range(n_gz - 1):
            copy_to(
                total, from_gz.at[k], gz_send.at[0], gz_recv.at[k], {"gz": 0}
            ).wait_recv()
        summed = sum((from_gz[k] for k in range(n_gz - 1)), total[...])

        def unfold(even, odd, spot):
            lower = even - odd
            for j in range(half):
                low[spot, half - 1 - j : half - j, :] = lower[j : j + 1, :]
            return jnp.concatenate([low[spot], even + odd], axis=0)

        src = [
            unfold(
                summed[c * half : (c + 1) * half], summed[(4 + c) * half : (5 + c) * half], c
            )
            for c in range(4)
        ]
        near_x = jnp.where(low_x, summed[128:129], 0.0)
        before = jnp.where(low_y, summed[129:130], 0.0)
        sides = [
            jnp.broadcast_to(
                jnp.sum(
                    jnp.where(lane16 == row16 + 16 * kind, before, 0.0), axis=1, keepdims=True
                ),
                (16, 128),
            )
            for kind in range(2)
        ]
        near_y = unfold(sides[0], sides[1], 4)
        last = depth - 1
        coef = chosen(2, m_buf[last])
        h_out[0, last] = h_out[0, last] - COURANT * src[2]
        h_out[1, last] = h_out[1, last] - COURANT * src[3]
        behind_x = src[3] - jnp.where(row == 0, near_x, pltpu.roll(src[3], 1, 0))
        behind_y = src[2] - jnp.where(lane == 0, near_y, pltpu.roll(src[2], 1, 1))
        e_out[0, last] = e_out[0, last] + coef * (COURANT * src[3] - src[0])
        e_out[1, last] = e_out[1, last] - coef * (COURANT * src[2] + src[1])
        e_out[2, last] = e_out[2, last] - coef * (COURANT * (behind_x - behind_y))

    def sent(other, carry):
        @pl.when(other != z)
        def _():
            share(other).wait_send()

        return carry

    lax.fori_loop(0, n_z, sent, 0)
    for k in range(1, n_x):
        to_x(k).wait_send()
    when(low_x, ex_copy.wait_send)
    when(low_y, ey_copy.wait_send)
    when(low_z, ez_copy.wait_send)
    when(high_x, hx_copy.wait_send)
    when(high_y, hy_copy.wait_send)
    when(high_z, hz_copy.wait_send)
    when(jnp.logical_not(is_top), to_top(gz).wait_send)


def local(
    sizes, e_field, h_field, pole_current, material, pole_table, cotangent, cosines, wavenumber,
    time_phase,
):
    n_lo, n_hi, n_x, n_gz = sizes
    n_z = n_lo * n_hi
    depth, width_x, width_y = material.shape
    half = width_x // 2
    block = (3, depth, width_x, width_y)
    vmem = pl.BlockSpec(memory_space=pltpu.VMEM)
    hbm = pl.BlockSpec(memory_space=pl.ANY)
    dma = pltpu.SemaphoreType.DMA
    cot = jnp.transpose(cotangent, (1, 2, 0))
    field = jax.ShapeDtypeStruct(block, F32)
    return tuple(
        pl.pallas_call(
            functools.partial(kernel, sizes),
            out_shape=(field, field, field),
            in_specs=[hbm] * 9,
            out_specs=(vmem, vmem, vmem),
            scratch_shapes=[
                pltpu.VMEM((8, 8, 16), F32),
                pltpu.SMEM((2, 8), F32),
                pltpu.SMEM((16,), F32),
                pltpu.SMEM((16,), F32),
                pltpu.SMEM((3, 4), F32),
                pltpu.VMEM(block, F32),
                pltpu.VMEM(block, F32),
                pltpu.VMEM(block, F32),
                pltpu.VMEM((depth, width_x, width_y), jnp.int32),
                pltpu.VMEM((n_z, 16, 128), F32),
                pltpu.VMEM((n_z // 2, 2, half, 128), F32),
                pltpu.VMEM((n_z // 2, 8, 128), F32),
                pltpu.VMEM((n_x, n_z // 2, 8, 128), F32),
                pltpu.VMEM((256, n_z * 128), BF16),
                pltpu.VMEM((288, n_z * 128), BF16),
                pltpu.VMEM((n_x, 136, 128), F32),
                pltpu.VMEM((n_x - 1, 136, 128), F32),
                pltpu.VMEM((136, 128), F32),
                pltpu.VMEM((n_gz - 1, 136, 128), F32),
                pltpu.VMEM((5, half, 128), F32),
                pltpu.VMEM((8, 128), F32),
                pltpu.VMEM((8, 128), F32),
                pltpu.VMEM((8, 128), F32),
                pltpu.VMEM((8, 128), F32),
                pltpu.VMEM((2, width_x, 128), F32),
                pltpu.VMEM((8, 128), F32),
                pltpu.VMEM((8, 128), F32),
                pltpu.VMEM((8, 128), F32),
                pltpu.VMEM((8, 128), F32),
                pltpu.VMEM((2, width_x, 128), F32),
                dma((9,)),
                dma((n_z,)),
                dma((n_z,)),
                dma((n_x - 1,)),
                dma((n_x - 1,)),
                dma((1,)),
                dma((n_gz - 1,)),
                dma((6,)),
                dma((6,)),
            ],
            compiler_params=pltpu.CompilerParams(
                collective_id=0, has_side_effects=True, vmem_limit_bytes=60 * 1024 * 1024
            ),
        )(cot, cosines, wavenumber, time_phase, pole_table, e_field, h_field, pole_current, material)
    )


def solution(mesh):
    sizes = (mesh.shape["gx"], PLANES, mesh.shape["gy"] // PLANES, mesh.shape["gz"])
    field = P(None, "gz", "gx", "gy")
    in_specs = (
        field,
        field,
        field,
        P("gz", "gx", "gy"),
        P(),
        P(None, None, ("gx", "gy", "gz")),
        P(None, ("gx", "gy", "gz")),
        P(),
        P(),
    )
    return jax.shard_map(
        functools.partial(local, sizes),
        mesh=mesh,
        in_specs=in_specs,
        out_specs=(field, field, field),
        check_vma=False,
    )
```

```python
import functools
import math

import jax
import jax.numpy as jnp
from jax import lax
from jax.experimental import pallas as pl
from jax.experimental.pallas import tpu as pltpu
from jax.sharding import PartitionSpec as P

PLANES = 4
COURANT = 0.5
MESH = pl.DeviceIdType.MESH
F32 = jnp.float32
BF16 = jnp.bfloat16

TURN = 2.0 * math.pi
TURN_HI = 6.28125
TURN_LO = TURN - TURN_HI


def sincos(phase):
    turns = jnp.floor(phase * (1.0 / TURN) + 0.5)
    rest = ((phase - turns * TURN_HI) - turns * TURN_LO) * 0.25
    sq = rest * rest
    sin = rest + rest * sq * (
        -1.6666654611e-1 + sq * (8.3321608736e-3 + sq * -1.9515295891e-4)
    )
    cos = 1.0 - 0.5 * sq + sq * sq * (
        4.166664568298827e-2 + sq * (-1.388731625493765e-3 + sq * 2.443315711809948e-5)
    )
    for _ in range(2):
        sin, cos = 2.0 * sin * cos, 1.0 - 2.0 * sin * sin
    return sin, cos


def times(a, b):
    return a[0] * b[0] - a[1] * b[1], a[0] * b[1] + a[1] * b[0]


def split(value):
    high = value.astype(BF16)
    return high, (value - high.astype(F32)).astype(BF16)


def iota(shape, dim):
    return lax.broadcasted_iota(jnp.int32, shape, dim)


def kernel(
    sizes, cot_in, cosines_in, wave_in, phase_in, table_in, e_in, h_in, p_in, m_in,
    e_out, h_out, p_out, cot, cosines, wave, phase, table, e_buf, h_buf, p_buf, m_buf,
    gat, xs, edge, pq, yt, lt, acc, from_x, total, from_gz, low,
    hx_out, hx_in, hy_out, hy_in, hz_in, kx_out, kx_in, ky_out, ky_in, kz_in,
    load_sem, gat_send, gat_recv, x_send, x_recv, gz_send, gz_recv, halo_send, halo_recv,
    x_token, top_token,
):
    n_lo, n_hi, n_x, n_gz = sizes
    n_z = n_lo * n_hi
    n_half = n_z // 2
    depth, width_x, width_y = m_buf.shape
    half = width_x // 2
    gx, gy, gz = lax.axis_index("gx"), lax.axis_index("gy"), lax.axis_index("gz")
    z_hi = gy & (n_hi - 1)
    x = gy // n_hi
    z = z_hi * n_lo + gx
    is_top = gz == n_gz - 1

    def plane(other):
        return {"gx": other & (n_lo - 1), "gy": x * n_hi + other // n_lo}

    def column_of(k):
        return {"gy": ((x + k) & (n_x - 1)) * n_hi + z_hi}

    def copy_to(src, dst, send_sem, recv_sem, device):
        return pltpu.make_async_remote_copy(
            src_ref=src, dst_ref=dst, send_sem=send_sem, recv_sem=recv_sem,
            device_id=device, device_id_type=MESH,
        )

    loads = [
        pltpu.make_async_copy(a, b, load_sem.at[i])
        for i, (a, b) in enumerate(
            (
                (cot_in, cot),
                (cosines_in, cosines),
                (wave_in, wave),
                (phase_in, phase),
                (e_in, e_buf),
                (h_in, h_buf),
                (p_in, p_buf),
                (m_in, m_buf),
                (table_in, table),
            )
        )
    ]
    for load in loads:
        load.start()

    wrap_low = jnp.logical_and(z_hi == n_hi - 1, x < n_x - 1)
    wrap_high = jnp.logical_and(z_hi == 0, x > 0)

    barrier = pltpu.get_barrier_semaphore()

    def greet(device):
        pl.semaphore_signal(barrier, inc=1, device_id=device, device_id_type=MESH)

    def greet_plane(other, carry):
        greet(plane(other))
        return carry

    lax.fori_loop(z + 1, n_z, greet_plane, 0)

    def greet_column(other, carry):
        greet({"gy": other * n_hi + z_hi})
        return carry

    lax.fori_loop(x + 1, n_x, greet_column, 0)

    @pl.when(gz < n_gz - 1)
    def _():
        greet({"gz": gz + 1})

    @pl.when(gz < n_gz - 2)
    def _():
        greet({"gz": n_gz - 1})

    @pl.when(wrap_high)
    def _():
        greet({"gy": gy - 1})

    greeted = (
        z
        + x
        + jnp.where(is_top, n_gz - 1, (gz > 0).astype(jnp.int32))
        + wrap_low.astype(jnp.int32)
    )

    for load in loads[:4]:
        load.wait()
    row8 = iota((8, 128), 0)
    lane8 = iota((8, 128), 1)
    lane1 = iota((1, 128), 1)
    freq = lane1 & 15
    direction = lane1 >> 4
    waves = jnp.zeros((1, 128), F32)
    delays = jnp.zeros((1, 128), F32)
    cos_x = jnp.zeros((1, 128), F32)
    cos_y = jnp.zeros((1, 128), F32)
    for f in range(16):
        waves = jnp.where(freq == f, wave[f], waves)
        delays = jnp.where(freq == f, phase[f], delays)
    for d in range(8):
        cos_x = jnp.where(direction == d, cosines[0, d], cos_x)
        cos_y = jnp.where(direction == d, cosines[1, d], cos_y)
    weights = jnp.concatenate([cot[:, d, :] for d in range(8)], axis=1)
    scale = 1.0 / math.sqrt(16.0 * 8 * n_lo * n_hi * n_x * n_gz)
    sin_t, cos_t = sincos(-delays)
    re = [weights[2 * c : 2 * c + 1] * scale for c in range(4)]
    im = [weights[2 * c + 1 : 2 * c + 2] * scale for c in range(4)]
    mine = gat.at[z]
    for c in range(4):
        mine[c : c + 1, :] = re[c] * cos_t - im[c] * sin_t
        mine[4 + c : 5 + c, :] = re[c] * sin_t + im[c] * cos_t
    mine[8:9, :] = waves * cos_x
    mine[9:10, :] = waves * cos_y

    @pl.when(greeted > 0)
    def _():
        pl.semaphore_wait(barrier, greeted)

    def share(other):
        block = gat.at[z, 0:10]
        return copy_to(block, block, gat_send.at[other], gat_recv.at[z], plane(other))

    def arrival(other):
        block = gat.at[other, 0:10]
        return copy_to(block, block, gat_send.at[other], gat_recv.at[other], plane(other))

    def share_down(other, carry):
        share(other).start()
        return carry

    lax.fori_loop(0, z, share_down, 0)

    def tell_column(other, carry):
        pl.semaphore_signal(
            x_token, inc=1, device_id={"gy": other * n_hi + z_hi}, device_id_type=MESH
        )
        return carry

    lax.fori_loop(0, x, tell_column, 0)

    @pl.when(is_top)
    def _():
        for k in range(n_gz - 1):
            pl.semaphore_signal(top_token, inc=1, device_id={"gz": k}, device_id_type=MESH)

    loads[4].wait()
    groups = width_x // 8
    low_x, high_x = gx > 0, gx < n_lo - 1
    low_z, high_z = gz > 0, gz < n_gz - 1
    low_y, high_y = gy > 0, gy < n_hi * n_x - 1
    plain_low_y, plain_high_y = z_hi > 0, z_hi < n_hi - 1
    ex_copy = copy_to(hx_out, hx_in, halo_send.at[0], halo_recv.at[0], {"gx": gx - 1})
    ey_copy = copy_to(hy_out, hy_in, halo_send.at[1], halo_recv.at[1], {"gy": gy - 1})
    ez_copy = copy_to(
        e_buf.at[0:2, 0], hz_in, halo_send.at[2], halo_recv.at[2], {"gz": gz - 1}
    )
    hx_copy = copy_to(kx_out, kx_in, halo_send.at[3], halo_recv.at[3], {"gx": gx + 1})
    hy_copy = copy_to(ky_out, ky_in, halo_send.at[4], halo_recv.at[4], {"gy": gy + 1})
    hz_copy = copy_to(
        h_buf.at[0:2, depth - 1], kz_in, halo_send.at[5], halo_recv.at[5], {"gz": gz + 1}
    )

    def when(flag, action):
        @pl.when(flag)
        def _():
            action()

    when(low_z, ez_copy.start)
    for i in range(2):
        for j in range(depth):
            hx_out[i * depth + j : i * depth + j + 1, :] = e_buf[1 + i, j, 0:1, :]
    when(low_x, ex_copy.start)
    packed = jnp.zeros((8, 128), F32)
    for i in range(2):
        for j in range(depth):
            for g in range(groups):
                to = (i * depth + j) * groups + g
                col = e_buf[2 * i, j, 8 * g : 8 * g + 8, :]
                packed = jnp.where(lane8 == to, pltpu.roll(col, to, 1) if to else col, packed)
    hy_out[...] = packed
    when(plain_low_y, ey_copy.start)

    def wait_for(other, carry):
        arrival(other).wait_recv()
        return carry

    def answer(other, carry):
        arrival(other).wait_recv()
        share(other).start()
        return carry

    def collect_own(first):
        lax.fori_loop(z + 1, first + n_half, answer, 0)
        lax.fori_loop(first, z, wait_for, 0)

    def collect_other(first):
        near_first = (z & (n_half - 1)) < n_half // 2

        def one(i, carry):
            other = jnp.where(near_first, first + (n_half - 1) - i, first + i)
            arrival(other).wait_recv()

            @pl.when(other > z)
            def _():
                share(other).start()

            return carry

        lax.fori_loop(0, n_half, one, 0)

    rowf = row8.astype(F32)
    centre = (gx * width_x).astype(F32) + (0.5 * width_x - 0.5)
    tile_y = ((row8 * n_hi + z_hi) * width_y).astype(F32)
    mul_x = jnp.where(
        row8 < 4, centre, jnp.where(row8 == 5, half + 0.5, jnp.where(row8 == 7, 8.0, 0.0))
    )
    mul_y = jnp.where(
        row8 < 4, tile_y, jnp.where(row8 == 4, 8.0, jnp.where(row8 == 6, 64.0, 0.0))
    )
    sign = jnp.where(row8 < 4, -1.0, 1.0)

    def factors_of(first):
        def factors(s, carry):
            along_x = gat[first + s, 8:9, :]
            along_y = gat[first + s, 9:10, :]
            w = gat[first + s, 0:8, :]
            turned = pltpu.roll(w, 4, 0) * sign
            sin_m, cos_m = sincos(along_x * mul_x + along_y * mul_y)
            for t in range(n_x):
                pq[t, s] = w * cos_m[t : t + 1] + turned * sin_m[t : t + 1]
            sin_b, cos_b = sincos(along_x * (rowf + 0.5))
            more = times((cos_b, sin_b), (cos_m[7:8], sin_m[7:8]))
            xs[s, 0, 0:8] = cos_b
            xs[s, 0, 8:16] = more[0]
            xs[s, 1, 0:8] = sin_b
            xs[s, 1, 8:16] = more[1]
            edge[s, 0:1] = cos_m[5:6]
            edge[s, 1:2] = -sin_m[5:6]
            sin_b, cos_b = sincos(along_y * rowf)
            edge[s, 2:3] = cos_b[1:2]
            edge[s, 3:4] = -sin_b[1:2]
            e8 = (cos_m[4:5], sin_m[4:5])
            e16 = times(e8, e8)
            more = times((cos_b, sin_b), e8)
            block = (jnp.concatenate([cos_b, more[0]], 0), jnp.concatenate([sin_b, more[1]], 0))
            blocks = [block]
            for power in (e16, times(e16, e16), (cos_m[6:7], sin_m[6:7])):
                blocks = blocks + [times(b, power) for b in blocks]
            for g, b in enumerate(blocks):
                for kind in range(2):
                    high, lowp = split(b[kind])
                    base = pl.multiple_of(s * 256 + kind * 128, 128)
                    yt[16 * g : 16 * g + 16, pl.ds(base, 128)] = high
                    yt[128 + 16 * g : 144 + 16 * g, pl.ds(base, 128)] = lowp
            return carry

        lax.fori_loop(0, n_half, factors, 0)

    row16 = iota((16, 128), 0)
    lane16 = iota((16, 128), 1)

    def tile(t):
        def build(s, cols):
            cx, sx = xs[s, 0], xs[s, 1]
            nx = -sx

            def put(r, k, value):
                high, lowp = split(value)
                base = pl.multiple_of(s * 256 + k * 128, 128)
                lt[r : r + 16, pl.ds(base, 128)] = high
                lt[144 + r : 160 + r, pl.ds(base, 128)] = lowp

            for c in range(4):
                p = pq[t, s, c : c + 1, :]
                nq = -pq[t, s, 4 + c : 5 + c, :]
                products = ((p * cx, nq * cx), (nq * sx, p * nx))
                for kind in range(2):
                    for k in range(2):
                        put((kind * 4 + c) * half, k, products[kind][k])
                if c == 2:
                    cy, sy = edge[s, 2:3, :], edge[s, 3:4, :]
                    cols = tuple(
                        old + (new[0] * cy + new[1] * sy) for old, new in zip(cols, products)
                    )
                if c == 3:
                    ox, oy = edge[s, 0:1, :], edge[s, 1:2, :]
                    put(128, 0, jnp.broadcast_to(p * ox + nq * oy, (16, 128)))
                    put(128, 1, jnp.broadcast_to(nq * ox - p * oy, (16, 128)))
            return cols

        zero = jnp.zeros((16, 128), F32)
        cols = lax.fori_loop(0, n_half, build, (zero, zero))
        both = lax.dot_general(
            lt[...], yt[...], (((1,), (1,)), ((), ())), preferred_element_type=F32
        )
        main = both[0:136, 0:128] + (both[0:136, 128:256] + both[144:280, 0:128])
        before = jnp.zeros((1, 128), F32)
        for kind in range(2):
            sums = jnp.sum(cols[kind], axis=1, keepdims=True)
            placed = jnp.where(lane16 == row16 + 16 * kind, sums, 0.0)
            before = before + jnp.sum(placed, axis=0, keepdims=True)
        return main[0:128], jnp.where(row8 == 0, main[128:136], jnp.where(row8 == 1, before, 0.0))

    own_half = (z // n_half) * n_half
    other_half = n_half - own_half
    collect_own(own_half)
    factors_of(own_half)

    def first_pass(k, carry):
        main, rest = tile((x + k) & (n_x - 1))
        acc[k, 0:128] = main
        acc[k, 128:136] = rest
        return carry

    lax.fori_loop(0, n_x, first_pass, 0)

    loads[5].wait()
    when(high_x, ex_copy.wait_recv)
    when(plain_high_y, ey_copy.wait_recv)
    when(high_z, ez_copy.wait_recv)
    row = iota((width_x, 128), 0)
    lane = iota((width_x, 128), 1)

    def column(packed, which, lane_to):
        cols = []
        for g in range(groups):
            by = (lane_to - which * groups - g) % 128
            cols.append(pltpu.roll(packed, by, 1) if by else packed)
        return jnp.concatenate(cols, axis=0)

    x_edges = jnp.where(high_x, hx_in[...], 0.0)
    y_packed = jnp.where(plain_high_y, hy_in[...], 0.0)
    z_edges = [jnp.where(high_z, hz_in[i], 0.0) for i in range(2)]
    for j in range(depth):
        ex, ey, ez = e_buf[0, j], e_buf[1, j], e_buf[2, j]
        ex_z, ey_z = (e_buf[0, j + 1], e_buf[1, j + 1]) if j < depth - 1 else z_edges

        def up_x(v, i):
            next_row = x_edges[i * depth + j : i * depth + j + 1, :]
            return jnp.where(row == width_x - 1, next_row, pltpu.roll(v, width_x - 1, 0)) - v

        def up_y(v, i):
            next_col = column(y_packed, i * depth + j, 127)
            return jnp.where(lane == 127, next_col, pltpu.roll(v, 127, 1)) - v

        h_buf[0, j] = h_buf[0, j] - COURANT * (up_y(ez, 1) - (ey_z - ey))
        h_buf[1, j] = h_buf[1, j] - COURANT * ((ex_z - ex) - up_x(ez, 1))
        h_buf[2, j] = h_buf[2, j] - COURANT * (up_x(ey, 0) - up_y(ex, 0))

    packed = jnp.zeros((8, 128), F32)
    for i in range(2):
        for j in range(depth):
            for g in range(groups):
                to = (i * depth + j) * groups + g
                col = h_buf[2 * i, j, 8 * g : 8 * g + 8, :]
                packed = jnp.where(lane8 == to, pltpu.roll(col, to + 1, 1), packed)
    ky_out[...] = packed
    when(high_y, hy_copy.start)

    def send_hx_hz():
        for i in range(2):
            for j in range(depth):
                kx_out[i * depth + j : i * depth + j + 1, :] = h_buf[
                    1 + i, j, width_x - 1 : width_x, :
                ]
        when(high_x, hx_copy.start)
        when(high_z, hz_copy.start)

    when(jnp.logical_not(wrap_low), send_hx_hz)

    collect_other(other_half)

    factors_of(other_half)

    def to_x(k):
        return copy_to(
            acc.at[k], from_x.at[k - 1], x_send.at[k - 1], x_recv.at[k - 1], column_of(k)
        )

    @pl.when(x < n_x - 1)
    def _():
        pl.semaphore_wait(x_token, n_x - 1 - x)

    def second_pass(i, carry):
        k = jnp.where(i == n_x - 1, 0, jnp.where(i == 0, n_x // 2, jnp.where(i == 1, 1, i + 1)))
        main, rest = tile((x + k) & (n_x - 1))
        acc[k, 0:128] = acc[k, 0:128] + main
        acc[k, 128:136] = acc[k, 128:136] + rest

        @pl.when(k > 0)
        def _():
            to_x(k).start()

        return carry

    lax.fori_loop(0, n_x, second_pass, 0)

    @pl.when(wrap_high)
    def _():
        hy_copy.wait_recv()
        ey_copy.start()

    @pl.when(wrap_low)
    def _():
        ey_copy.wait_recv()
        late = hy_in[...]
        for j in range(depth):
            h_buf[0, j] = h_buf[0, j] - jnp.where(
                lane == 127, COURANT * column(late, depth + j, 127), 0.0
            )
            h_buf[2, j] = h_buf[2, j] + jnp.where(
                lane == 127, COURANT * column(late, j, 127), 0.0
            )
        send_hx_hz()

    for load in loads[6:]:
        load.wait()
    when(low_x, hx_copy.wait_recv)
    when(plain_low_y, hy_copy.wait_recv)
    when(low_z, hz_copy.wait_recv)
    x_edges = jnp.where(low_x, kx_in[...], 0.0)
    y_packed = jnp.where(low_y, ky_in[...], 0.0)
    z_edges = [jnp.where(low_z, kz_in[i], 0.0) for i in range(2)]
    missing = jnp.where(wrap_high, COURANT, 0.0)

    def chosen(which, m):
        value = jnp.full(m.shape, table[which, 3], F32)
        for i in range(3):
            value = jnp.where(m == i, table[which, i], value)
        return value

    for j in range(depth):
        hx, hy, hz = h_buf[0, j], h_buf[1, j], h_buf[2, j]
        hx_z, hy_z = (h_buf[0, j - 1], h_buf[1, j - 1]) if j > 0 else z_edges
        ex, ey, ez = e_buf[0, j], e_buf[1, j], e_buf[2, j]

        def down_x(v, i):
            last_row = x_edges[i * depth + j : i * depth + j + 1, :]
            return v - jnp.where(row == 0, last_row, pltpu.roll(v, 1, 0))

        def down_y(v, i, rest):
            last_col = column(y_packed, i * depth + j, 0) + rest
            return v - jnp.where(lane == 0, last_col, pltpu.roll(v, 1, 1))

        side = (
            down_y(hz, 1, missing * ex) - (hy - hy_z),
            (hx - hx_z) - down_x(hz, 1),
            down_x(hy, 0) - down_y(hx, 0, -missing * ez),
        )
        m = m_buf[j]
        decay, drive, coef = chosen(0, m), chosen(1, m), chosen(2, m)
        for i, e in enumerate((ex, ey, ez)):
            pole = p_buf[i, j]
            after = decay * pole + drive * e
            p_out[i, j] = after
            e_out[i, j] = e + coef * (side[i] - 0.5 * (after + pole))
            h_out[i, j] = h_buf[i, j]

    for k in range(1, n_x):
        to_x(k).wait_recv()
    total[...] = sum((from_x[k] for k in range(n_x - 1)), acc[0])

    def to_top(k):
        return copy_to(
            total, from_gz.at[k], gz_send.at[0], gz_recv.at[k], {"gz": n_gz - 1}
        )

    @pl.when(jnp.logical_not(is_top))
    def _():
        pl.semaphore_wait(top_token, 1)
        to_top(gz).start()

    @pl.when(is_top)
    def _():
        for k in range(n_gz - 1):
            copy_to(
                total, from_gz.at[k], gz_send.at[0], gz_recv.at[k], {"gz": 0}
            ).wait_recv()
        summed = sum((from_gz[k] for k in range(n_gz - 1)), total[...])

        def unfold(even, odd, spot):
            lower = even - odd
            for j in range(half):
                low[spot, half - 1 - j : half - j, :] = lower[j : j + 1, :]
            return jnp.concatenate([low[spot], even + odd], axis=0)

        src = [
            unfold(
                summed[c * half : (c + 1) * half], summed[(4 + c) * half : (5 + c) * half], c
            )
            for c in range(4)
        ]
        near_x = jnp.where(low_x, summed[128:129], 0.0)
        before = jnp.where(low_y, summed[129:130], 0.0)
        sides = [
            jnp.broadcast_to(
                jnp.sum(
                    jnp.where(lane16 == row16 + 16 * kind, before, 0.0), axis=1, keepdims=True
                ),
                (16, 128),
            )
            for kind in range(2)
        ]
        near_y = unfold(sides[0], sides[1], 4)
        last = depth - 1
        coef = chosen(2, m_buf[last])
        h_out[0, last] = h_out[0, last] - COURANT * src[2]
        h_out[1, last] = h_out[1, last] - COURANT * src[3]
        behind_x = src[3] - jnp.where(row == 0, near_x, pltpu.roll(src[3], 1, 0))
        behind_y = src[2] - jnp.where(lane == 0, near_y, pltpu.roll(src[2], 1, 1))
        e_out[0, last] = e_out[0, last] + coef * (COURANT * src[3] - src[0])
        e_out[1, last] = e_out[1, last] - coef * (COURANT * src[2] + src[1])
        e_out[2, last] = e_out[2, last] - coef * (COURANT * (behind_x - behind_y))

    def sent(other, carry):
        @pl.when(other != z)
        def _():
            share(other).wait_send()

        return carry

    lax.fori_loop(0, n_z, sent, 0)
    for k in range(1, n_x):
        to_x(k).wait_send()
    when(low_x, ex_copy.wait_send)
    when(low_y, ey_copy.wait_send)
    when(low_z, ez_copy.wait_send)
    when(high_x, hx_copy.wait_send)
    when(high_y, hy_copy.wait_send)
    when(high_z, hz_copy.wait_send)
    when(jnp.logical_not(is_top), to_top(gz).wait_send)


def put(*refs):
    for src, dst in zip(refs[:3], refs[3:]):
        dst[...] = src[...]


def local(
    sizes, e_field, h_field, pole_current, material, pole_table, cotangent, cosines, wavenumber,
    time_phase,
):
    n_lo, n_hi, n_x, n_gz = sizes
    n_z = n_lo * n_hi
    depth, width_x, width_y = material.shape
    half = width_x // 2
    block = (3, depth, width_x, width_y)
    vmem = pl.BlockSpec(memory_space=pltpu.VMEM)
    hbm = pl.BlockSpec(memory_space=pl.ANY)
    dma = pltpu.SemaphoreType.DMA
    cot = jnp.transpose(cotangent, (1, 2, 0))
    field = jax.ShapeDtypeStruct(block, F32)
    results = pl.pallas_call(
        functools.partial(kernel, sizes),
        out_shape=(field, field, field),
        in_specs=[hbm] * 9,
        out_specs=(vmem, vmem, vmem),
        scratch_shapes=[
            pltpu.VMEM((8, 8, 16), F32),
            pltpu.SMEM((2, 8), F32),
            pltpu.SMEM((16,), F32),
            pltpu.SMEM((16,), F32),
            pltpu.SMEM((3, 4), F32),
            pltpu.VMEM(block, F32),
            pltpu.VMEM(block, F32),
            pltpu.VMEM(block, F32),
            pltpu.VMEM((depth, width_x, width_y), jnp.int32),
            pltpu.VMEM((n_z, 16, 128), F32),
            pltpu.VMEM((n_z // 2, 2, half, 128), F32),
            pltpu.VMEM((n_z // 2, 8, 128), F32),
            pltpu.VMEM((n_x, n_z // 2, 8, 128), F32),
            pltpu.VMEM((256, n_z * 128), BF16),
            pltpu.VMEM((288, n_z * 128), BF16),
            pltpu.VMEM((n_x, 136, 128), F32),
            pltpu.VMEM((n_x - 1, 136, 128), F32),
            pltpu.VMEM((136, 128), F32),
            pltpu.VMEM((n_gz - 1, 136, 128), F32),
            pltpu.VMEM((5, half, 128), F32),
            pltpu.VMEM((8, 128), F32),
            pltpu.VMEM((8, 128), F32),
            pltpu.VMEM((8, 128), F32),
            pltpu.VMEM((8, 128), F32),
            pltpu.VMEM((2, width_x, 128), F32),
            pltpu.VMEM((8, 128), F32),
            pltpu.VMEM((8, 128), F32),
            pltpu.VMEM((8, 128), F32),
            pltpu.VMEM((8, 128), F32),
            pltpu.VMEM((2, width_x, 128), F32),
            dma((9,)),
            dma((n_z,)),
            dma((n_z,)),
            dma((n_x - 1,)),
            dma((n_x - 1,)),
            dma((1,)),
            dma((n_gz - 1,)),
            dma((6,)),
            dma((6,)),
            pltpu.SemaphoreType.REGULAR,
            pltpu.SemaphoreType.REGULAR,
        ],
        compiler_params=pltpu.CompilerParams(
            collective_id=0, has_side_effects=True, vmem_limit_bytes=60 * 1024 * 1024
        ),
    )(cot, cosines, wavenumber, time_phase, pole_table, e_field, h_field, pole_current, material)
    return tuple(
        pl.pallas_call(
            put,
            out_shape=(field, field, field),
            in_specs=[vmem] * 3,
            out_specs=(vmem,) * 3,
            compiler_params=pltpu.CompilerParams(vmem_limit_bytes=60 * 1024 * 1024),
        )(*results)
    )


def solution(mesh):
    sizes = (mesh.shape["gx"], PLANES, mesh.shape["gy"] // PLANES, mesh.shape["gz"])
    field = P(None, "gz", "gx", "gy")
    in_specs = (
        field,
        field,
        field,
        P("gz", "gx", "gy"),
        P(),
        P(None, None, ("gx", "gy", "gz")),
        P(None, ("gx", "gy", "gz")),
        P(),
        P(),
    )
    return jax.shard_map(
        functools.partial(local, sizes),
        mesh=mesh,
        in_specs=in_specs,
        out_specs=(field, field, field),
        check_vma=False,
    )
```

```python
import functools
import math

import jax
import jax.numpy as jnp
from jax import lax
from jax.experimental import pallas as pl
from jax.experimental.pallas import tpu as pltpu
from jax.sharding import PartitionSpec as P

PLANES = 4
COURANT = 0.5
MESH = pl.DeviceIdType.MESH
F32 = jnp.float32
BF16 = jnp.bfloat16

TURN = 2.0 * math.pi
TURN_HI = 6.28125
TURN_LO = TURN - TURN_HI


def sincos(phase):
    turns = jnp.floor(phase * (1.0 / TURN) + 0.5)
    rest = ((phase - turns * TURN_HI) - turns * TURN_LO) * 0.25
    sq = rest * rest
    sin = rest + rest * sq * (
        -1.6666654611e-1 + sq * (8.3321608736e-3 + sq * -1.9515295891e-4)
    )
    cos = 1.0 - 0.5 * sq + sq * sq * (
        4.166664568298827e-2 + sq * (-1.388731625493765e-3 + sq * 2.443315711809948e-5)
    )
    for _ in range(2):
        sin, cos = 2.0 * sin * cos, 1.0 - 2.0 * sin * sin
    return sin, cos


def times(a, b):
    return a[0] * b[0] - a[1] * b[1], a[0] * b[1] + a[1] * b[0]


def split(value):
    high = value.astype(BF16)
    return high, (value - high.astype(F32)).astype(BF16)


def iota(shape, dim):
    return lax.broadcasted_iota(jnp.int32, shape, dim)


def kernel(
    sizes, cot_in, cosines_in, wave_in, phase_in, table_in, e_in, h_in, p_in, m_in,
    e_out, h_out, p_out, cot, cosines, wave, phase, table, e_buf, h_buf, p_buf, m_buf,
    gat, yt, lt, cols, acc, from_x, total, from_gz, low,
    hx_out, hx_in, hy_out, hy_in, hz_in, kx_out, kx_in, ky_out, ky_in, kz_in,
    load_sem, gat_send, gat_recv, x_send, x_recv, gz_send, gz_recv, halo_send, halo_recv,
    x_token, top_token,
):
    n_lo, n_hi, n_x, n_gz = sizes
    n_z = n_lo * n_hi
    n_half = n_z // 2
    depth, width_x, width_y = m_buf.shape
    half = width_x // 2
    gx, gy, gz = lax.axis_index("gx"), lax.axis_index("gy"), lax.axis_index("gz")
    z_hi = gy & (n_hi - 1)
    x = gy // n_hi
    def swap(k):
        return jnp.where(k < n_half, k, n_z + n_half - 1 - k)

    z = swap(z_hi * n_lo + gx)
    is_late = z >= n_half
    is_top = gz == n_gz - 1

    def plane(other):
        other = swap(other)
        return {"gx": other & (n_lo - 1), "gy": x * n_hi + other // n_lo}

    def column_of(k):
        return {"gy": ((x + k) & (n_x - 1)) * n_hi + z_hi}

    def copy_to(src, dst, send_sem, recv_sem, device):
        return pltpu.make_async_remote_copy(
            src_ref=src, dst_ref=dst, send_sem=send_sem, recv_sem=recv_sem,
            device_id=device, device_id_type=MESH,
        )

    loads = [
        pltpu.make_async_copy(a, b, load_sem.at[i])
        for i, (a, b) in enumerate(
            (
                (cot_in, cot),
                (cosines_in, cosines),
                (wave_in, wave),
                (phase_in, phase),
                (e_in, e_buf),
                (h_in, h_buf),
                (p_in, p_buf),
                (m_in, m_buf),
                (table_in, table),
            )
        )
    ]
    for load in loads:
        load.start()

    wrap_low = jnp.logical_and(z_hi == n_hi - 1, x < n_x - 1)
    wrap_high = jnp.logical_and(z_hi == 0, x > 0)

    barrier = pltpu.get_barrier_semaphore()

    def greet(device):
        pl.semaphore_signal(barrier, inc=1, device_id=device, device_id_type=MESH)

    def greet_plane(other, carry):
        greet(plane(other))
        return carry

    lax.fori_loop(z + 1, n_z, greet_plane, 0)

    def greet_column(other, carry):
        greet({"gy": other * n_hi + z_hi})
        return carry

    lax.fori_loop(x + 1, n_x, greet_column, 0)

    @pl.when(gz < n_gz - 1)
    def _():
        greet({"gz": gz + 1})

    @pl.when(gz < n_gz - 2)
    def _():
        greet({"gz": n_gz - 1})

    @pl.when(wrap_high)
    def _():
        greet({"gy": gy - 1})

    @pl.when(jnp.logical_and(is_late, gx < n_lo - 1))
    def _():
        greet({"gx": gx + 1})

    @pl.when(jnp.logical_and(is_late, z_hi < n_hi - 1))
    def _():
        greet({"gy": gy + 1})

    greeted = (
        jnp.logical_and(is_late, gx > 0).astype(jnp.int32)
        + (z_hi > n_hi // 2).astype(jnp.int32)
        + z
        + x
        + jnp.where(is_top, n_gz - 1, (gz > 0).astype(jnp.int32))
        + wrap_low.astype(jnp.int32)
    )

    for load in loads[:4]:
        load.wait()
    row8 = iota((8, 128), 0)
    lane8 = iota((8, 128), 1)
    lane1 = iota((1, 128), 1)
    freq = lane1 & 15
    direction = lane1 >> 4
    waves = jnp.zeros((1, 128), F32)
    delays = jnp.zeros((1, 128), F32)
    cos_x = jnp.zeros((1, 128), F32)
    cos_y = jnp.zeros((1, 128), F32)
    for f in range(16):
        waves = jnp.where(freq == f, wave[f], waves)
        delays = jnp.where(freq == f, phase[f], delays)
    for d in range(8):
        cos_x = jnp.where(direction == d, cosines[0, d], cos_x)
        cos_y = jnp.where(direction == d, cosines[1, d], cos_y)
    weights = jnp.concatenate([cot[:, d, :] for d in range(8)], axis=1)
    scale = 1.0 / math.sqrt(16.0 * 8 * n_lo * n_hi * n_x * n_gz)
    sin_t, cos_t = sincos(-delays)
    re = [weights[2 * c : 2 * c + 1] * scale for c in range(4)]
    im = [weights[2 * c + 1 : 2 * c + 2] * scale for c in range(4)]
    mine = gat.at[z]
    for c in range(4):
        mine[c : c + 1, :] = re[c] * cos_t - im[c] * sin_t
        mine[4 + c : 5 + c, :] = re[c] * sin_t + im[c] * cos_t
    mine[8:9, :] = waves * cos_x
    mine[9:10, :] = waves * cos_y

    @pl.when(greeted > 0)
    def _():
        pl.semaphore_wait(barrier, greeted)

    def share(other):
        block = gat.at[z, 0:10]
        return copy_to(block, block, gat_send.at[other], gat_recv.at[z], plane(other))

    def arrival(other):
        block = gat.at[other, 0:10]
        return copy_to(block, block, gat_send.at[other], gat_recv.at[other], plane(other))

    def share_down(other, carry):
        share(other).start()
        return carry

    lax.fori_loop(0, z, share_down, 0)

    def tell_column(other, carry):
        pl.semaphore_signal(
            x_token, inc=1, device_id={"gy": other * n_hi + z_hi}, device_id_type=MESH
        )
        return carry

    lax.fori_loop(0, x, tell_column, 0)

    @pl.when(is_top)
    def _():
        for k in range(n_gz - 1):
            pl.semaphore_signal(top_token, inc=1, device_id={"gz": k}, device_id_type=MESH)

    loads[4].wait()
    groups = width_x // 8
    low_x, high_x = gx > 0, gx < n_lo - 1
    low_z, high_z = gz > 0, gz < n_gz - 1
    low_y, high_y = gy > 0, gy < n_hi * n_x - 1
    plain_low_y, plain_high_y = z_hi > 0, z_hi < n_hi - 1
    ex_copy = copy_to(hx_out, hx_in, halo_send.at[0], halo_recv.at[0], {"gx": gx - 1})
    ey_copy = copy_to(hy_out, hy_in, halo_send.at[1], halo_recv.at[1], {"gy": gy - 1})
    ez_copy = copy_to(
        e_buf.at[0:2, 0], hz_in, halo_send.at[2], halo_recv.at[2], {"gz": gz - 1}
    )
    hx_copy = copy_to(kx_out, kx_in, halo_send.at[3], halo_recv.at[3], {"gx": gx + 1})
    hy_copy = copy_to(ky_out, ky_in, halo_send.at[4], halo_recv.at[4], {"gy": gy + 1})
    hz_copy = copy_to(
        h_buf.at[0:2, depth - 1], kz_in, halo_send.at[5], halo_recv.at[5], {"gz": gz + 1}
    )

    def when(flag, action):
        @pl.when(flag)
        def _():
            action()

    when(low_z, ez_copy.start)
    for i in range(2):
        for j in range(depth):
            hx_out[i * depth + j : i * depth + j + 1, :] = e_buf[1 + i, j, 0:1, :]
    when(low_x, ex_copy.start)
    packed = jnp.zeros((8, 128), F32)
    for i in range(2):
        for j in range(depth):
            for g in range(groups):
                to = (i * depth + j) * groups + g
                col = e_buf[2 * i, j, 8 * g : 8 * g + 8, :]
                packed = jnp.where(lane8 == to, pltpu.roll(col, to, 1) if to else col, packed)
    hy_out[...] = packed
    when(plain_low_y, ey_copy.start)

    row = iota((width_x, 128), 0)
    lane = iota((width_x, 128), 1)

    def column(packed, which, lane_to):
        cols = []
        for g in range(groups):
            by = (lane_to - which * groups - g) % 128
            cols.append(pltpu.roll(packed, by, 1) if by else packed)
        return jnp.concatenate(cols, axis=0)

    def send_hx_hz():
        for i in range(2):
            for j in range(depth):
                kx_out[i * depth + j : i * depth + j + 1, :] = h_buf[
                    1 + i, j, width_x - 1 : width_x, :
                ]
        when(high_x, hx_copy.start)
        when(high_z, hz_copy.start)

    def magnetic():
        loads[5].wait()
        when(high_x, ex_copy.wait_recv)
        when(plain_high_y, ey_copy.wait_recv)
        when(high_z, ez_copy.wait_recv)
        x_edges = jnp.where(high_x, hx_in[...], 0.0)
        y_packed = jnp.where(plain_high_y, hy_in[...], 0.0)
        z_edges = [jnp.where(high_z, hz_in[i], 0.0) for i in range(2)]
        for j in range(depth):
            ex, ey, ez = e_buf[0, j], e_buf[1, j], e_buf[2, j]
            ex_z, ey_z = (e_buf[0, j + 1], e_buf[1, j + 1]) if j < depth - 1 else z_edges

            def up_x(v, i):
                next_row = x_edges[i * depth + j : i * depth + j + 1, :]
                return jnp.where(row == width_x - 1, next_row, pltpu.roll(v, width_x - 1, 0)) - v

            def up_y(v, i):
                next_col = column(y_packed, i * depth + j, 127)
                return jnp.where(lane == 127, next_col, pltpu.roll(v, 127, 1)) - v

            h_buf[0, j] = h_buf[0, j] - COURANT * (up_y(ez, 1) - (ey_z - ey))
            h_buf[1, j] = h_buf[1, j] - COURANT * ((ex_z - ex) - up_x(ez, 1))
            h_buf[2, j] = h_buf[2, j] - COURANT * (up_x(ey, 0) - up_y(ex, 0))

        packed = jnp.zeros((8, 128), F32)
        for i in range(2):
            for j in range(depth):
                for g in range(groups):
                    to = (i * depth + j) * groups + g
                    col = h_buf[2 * i, j, 8 * g : 8 * g + 8, :]
                    packed = jnp.where(lane8 == to, pltpu.roll(col, to + 1, 1), packed)
        ky_out[...] = packed
        when(high_y, hy_copy.start)

        when(jnp.logical_not(wrap_low), send_hx_hz)

    when(is_late, magnetic)

    rowf = row8.astype(F32)
    centre = (gx * width_x).astype(F32) + (0.5 * width_x - 0.5)
    tile_y = ((row8 * n_hi + z_hi) * width_y).astype(F32)
    mul_x = jnp.where(
        row8 < 4, centre, jnp.where(row8 == 5, half + 0.5, jnp.where(row8 == 7, 8.0, 0.0))
    )
    mul_y = jnp.where(
        row8 < 4, tile_y, jnp.where(row8 == 4, 8.0, jnp.where(row8 == 6, 64.0, 0.0))
    )
    sign = jnp.where(row8 < 4, -1.0, 1.0)

    row16 = iota((16, 128), 0)
    lane16 = iota((16, 128), 1)

    def operands(rank, s):
        along_x = gat[rank, 8:9, :]
        along_y = gat[rank, 9:10, :]
        w = gat[rank, 0:8, :]
        turned = pltpu.roll(w, 4, 0) * sign
        sin_m, cos_m = sincos(along_x * mul_x + along_y * mul_y)

        def spot(k):
            return pl.ds(pl.multiple_of(s * 256 + k * 128, 128), 128)

        sin_b, cos_b = sincos(along_y * rowf)
        before_y = (cos_b[1:2], -sin_b[1:2])
        e8 = (cos_m[4:5], sin_m[4:5])
        e16 = times(e8, e8)
        more = times((cos_b, sin_b), e8)
        blocks = [(jnp.concatenate([cos_b, more[0]], 0), jnp.concatenate([sin_b, more[1]], 0))]
        for power in (e16, times(e16, e16), (cos_m[6:7], sin_m[6:7])):
            blocks = blocks + [times(b, power) for b in blocks]
        for g, b in enumerate(blocks):
            for kind in range(2):
                high, lowp = split(b[kind])
                yt[16 * g : 16 * g + 16, spot(kind)] = high
                yt[128 + 16 * g : 144 + 16 * g, spot(kind)] = lowp

        sin_b, cos_b = sincos(along_x * (rowf + 0.5))
        more = times((cos_b, sin_b), (cos_m[7:8], sin_m[7:8]))
        cx = jnp.concatenate([cos_b, more[0]], 0)
        sx = jnp.concatenate([sin_b, more[1]], 0)
        nx = -sx
        before_x = (cos_m[5:6], -sin_m[5:6])
        for t in range(n_x):
            pq = w * cos_m[t : t + 1] + turned * sin_m[t : t + 1]

            def put_left(r, k, value):
                high, lowp = split(value)
                lt[t, r : r + 16, spot(k)] = high
                lt[t, 144 + r : 160 + r, spot(k)] = lowp

            for c in range(4):
                p = pq[c : c + 1, :]
                nq = -pq[4 + c : 5 + c, :]
                products = ((p * cx, nq * cx), (nq * sx, p * nx))
                for kind in range(2):
                    for k in range(2):
                        put_left((kind * 4 + c) * half, k, products[kind][k])
                if c == 2:
                    for kind in range(2):
                        cols[t, kind] = cols[t, kind] + (
                            products[kind][0] * before_y[0] + products[kind][1] * before_y[1]
                        )
                if c == 3:
                    ox, oy = before_x
                    put_left(128, 0, jnp.broadcast_to(p * ox + nq * oy, (16, 128)))
                    put_left(128, 1, jnp.broadcast_to(nq * ox - p * oy, (16, 128)))

    def answer(other, carry):
        arrival(other).wait_recv()
        share(other).start()
        return carry

    def answer_late():
        def one(i, carry):
            return answer(jnp.where(is_far, n_z - 1 - i, n_half + i), carry)

        lax.fori_loop(0, n_half, one, 0)

    def own_planes(i, carry):
        other = own_half + ((z + 1 + i) & (n_half - 1))

        @pl.when(jnp.logical_or(other < z, jnp.logical_and(other > z, jnp.logical_not(is_far))))
        def _():
            arrival(other).wait_recv()

        @pl.when(jnp.logical_and(other > z, jnp.logical_not(is_far)))
        def _():
            share(other).start()

        operands(other, other - own_half)
        return carry

    def other_planes(i, carry):
        @pl.when(is_late)
        def _():
            arrival(i).wait_recv()

        operands(other_half + i, i)
        return carry

    def tile(t):
        both = lax.dot_general(
            lt[t], yt[...], (((1,), (1,)), ((), ())), preferred_element_type=F32
        )
        main = both[0:136, 0:128] + (both[0:136, 128:256] + both[144:280, 0:128])
        before = jnp.zeros((1, 128), F32)
        for kind in range(2):
            sums = jnp.sum(cols[t, kind], axis=1, keepdims=True)
            placed = jnp.where(lane16 == row16 + 16 * kind, sums, 0.0)
            before = before + jnp.sum(placed, axis=0, keepdims=True)
        cols[t] = jnp.zeros((2, 16, 128), F32)
        return main[0:128], jnp.where(row8 == 0, main[128:136], jnp.where(row8 == 1, before, 0.0))

    cols[...] = jnp.zeros(cols.shape, F32)
    own_half = (z // n_half) * n_half
    other_half = n_half - own_half
    is_far = jnp.logical_and(z >= n_half // 2, jnp.logical_not(is_late))

    @pl.when(is_far)
    def _():
        lax.fori_loop(z + 1, n_half, answer, 0)
        answer_late()

    lax.fori_loop(0, n_half, own_planes, 0)

    def first_pass(k, carry):
        main, rest = tile((x + k) & (n_x - 1))
        acc[k, 0:128] = main
        acc[k, 128:136] = rest
        return carry

    lax.fori_loop(0, n_x, first_pass, 0)

    when(jnp.logical_not(is_late), magnetic)
    when(z < n_half // 2, answer_late)
    lax.fori_loop(0, n_half, other_planes, 0)

    def to_x(k):
        return copy_to(
            acc.at[k], from_x.at[k - 1], x_send.at[k - 1], x_recv.at[k - 1], column_of(k)
        )

    @pl.when(x < n_x - 1)
    def _():
        pl.semaphore_wait(x_token, n_x - 1 - x)

    def second_pass(i, carry):
        k = jnp.where(i == n_x - 1, 0, jnp.where(i == 0, n_x // 2, jnp.where(i == 1, 1, i + 1)))
        main, rest = tile((x + k) & (n_x - 1))
        acc[k, 0:128] = acc[k, 0:128] + main
        acc[k, 128:136] = acc[k, 128:136] + rest

        @pl.when(k > 0)
        def _():
            to_x(k).start()

        return carry

    lax.fori_loop(0, n_x, second_pass, 0)

    @pl.when(wrap_high)
    def _():
        hy_copy.wait_recv()
        ey_copy.start()

    @pl.when(wrap_low)
    def _():
        ey_copy.wait_recv()
        late = hy_in[...]
        for j in range(depth):
            h_buf[0, j] = h_buf[0, j] - jnp.where(
                lane == 127, COURANT * column(late, depth + j, 127), 0.0
            )
            h_buf[2, j] = h_buf[2, j] + jnp.where(
                lane == 127, COURANT * column(late, j, 127), 0.0
            )
        send_hx_hz()

    for k in range(1, n_x):
        to_x(k).wait_recv()
    total[...] = sum((from_x[k] for k in range(n_x - 1)), acc[0])

    def to_top(k):
        return copy_to(
            total, from_gz.at[k], gz_send.at[0], gz_recv.at[k], {"gz": n_gz - 1}
        )

    @pl.when(jnp.logical_not(is_top))
    def _():
        pl.semaphore_wait(top_token, 1)
        to_top(gz).start()

    for load in loads[6:]:
        load.wait()
    when(low_x, hx_copy.wait_recv)
    when(plain_low_y, hy_copy.wait_recv)
    when(low_z, hz_copy.wait_recv)
    x_edges = jnp.where(low_x, kx_in[...], 0.0)
    y_packed = jnp.where(low_y, ky_in[...], 0.0)
    z_edges = [jnp.where(low_z, kz_in[i], 0.0) for i in range(2)]
    missing = jnp.where(wrap_high, COURANT, 0.0)

    def chosen(which, m):
        value = jnp.full(m.shape, table[which, 3], F32)
        for i in range(3):
            value = jnp.where(m == i, table[which, i], value)
        return value

    for j in range(depth):
        hx, hy, hz = h_buf[0, j], h_buf[1, j], h_buf[2, j]
        hx_z, hy_z = (h_buf[0, j - 1], h_buf[1, j - 1]) if j > 0 else z_edges
        ex, ey, ez = e_buf[0, j], e_buf[1, j], e_buf[2, j]

        def down_x(v, i):
            last_row = x_edges[i * depth + j : i * depth + j + 1, :]
            return v - jnp.where(row == 0, last_row, pltpu.roll(v, 1, 0))

        def down_y(v, i, rest):
            last_col = column(y_packed, i * depth + j, 0) + rest
            return v - jnp.where(lane == 0, last_col, pltpu.roll(v, 1, 1))

        side = (
            down_y(hz, 1, missing * ex) - (hy - hy_z),
            (hx - hx_z) - down_x(hz, 1),
            down_x(hy, 0) - down_y(hx, 0, -missing * ez),
        )
        m = m_buf[j]
        decay, drive, coef = chosen(0, m), chosen(1, m), chosen(2, m)
        for i, e in enumerate((ex, ey, ez)):
            pole = p_buf[i, j]
            after = decay * pole + drive * e
            p_out[i, j] = after
            e_out[i, j] = e + coef * (side[i] - 0.5 * (after + pole))
            h_out[i, j] = h_buf[i, j]

    @pl.when(is_top)
    def _():
        for k in range(n_gz - 1):
            copy_to(
                total, from_gz.at[k], gz_send.at[0], gz_recv.at[k], {"gz": 0}
            ).wait_recv()
        summed = sum((from_gz[k] for k in range(n_gz - 1)), total[...])

        def unfold(even, odd, spot):
            lower = even - odd
            for j in range(half):
                low[spot, half - 1 - j : half - j, :] = lower[j : j + 1, :]
            return jnp.concatenate([low[spot], even + odd], axis=0)

        src = [
            unfold(
                summed[c * half : (c + 1) * half], summed[(4 + c) * half : (5 + c) * half], c
            )
            for c in range(4)
        ]
        near_x = jnp.where(low_x, summed[128:129], 0.0)
        before = jnp.where(low_y, summed[129:130], 0.0)
        sides = [
            jnp.broadcast_to(
                jnp.sum(
                    jnp.where(lane16 == row16 + 16 * kind, before, 0.0), axis=1, keepdims=True
                ),
                (16, 128),
            )
            for kind in range(2)
        ]
        near_y = unfold(sides[0], sides[1], 4)
        last = depth - 1
        coef = chosen(2, m_buf[last])
        h_out[0, last] = h_out[0, last] - COURANT * src[2]
        h_out[1, last] = h_out[1, last] - COURANT * src[3]
        behind_x = src[3] - jnp.where(row == 0, near_x, pltpu.roll(src[3], 1, 0))
        behind_y = src[2] - jnp.where(lane == 0, near_y, pltpu.roll(src[2], 1, 1))
        e_out[0, last] = e_out[0, last] + coef * (COURANT * src[3] - src[0])
        e_out[1, last] = e_out[1, last] - coef * (COURANT * src[2] + src[1])
        e_out[2, last] = e_out[2, last] - coef * (COURANT * (behind_x - behind_y))

    def sent(other, carry):
        @pl.when(other != z)
        def _():
            share(other).wait_send()

        return carry

    lax.fori_loop(0, n_z, sent, 0)
    for k in range(1, n_x):
        to_x(k).wait_send()
    when(low_x, ex_copy.wait_send)
    when(low_y, ey_copy.wait_send)
    when(low_z, ez_copy.wait_send)
    when(high_x, hx_copy.wait_send)
    when(high_y, hy_copy.wait_send)
    when(high_z, hz_copy.wait_send)
    when(jnp.logical_not(is_top), to_top(gz).wait_send)


def put(*refs):
    for src, dst in zip(refs[:3], refs[3:]):
        dst[...] = src[...]


def local(
    sizes, e_field, h_field, pole_current, material, pole_table, cotangent, cosines, wavenumber,
    time_phase,
):
    n_lo, n_hi, n_x, n_gz = sizes
    n_z = n_lo * n_hi
    depth, width_x, width_y = material.shape
    half = width_x // 2
    block = (3, depth, width_x, width_y)
    vmem = pl.BlockSpec(memory_space=pltpu.VMEM)
    hbm = pl.BlockSpec(memory_space=pl.ANY)
    dma = pltpu.SemaphoreType.DMA
    cot = jnp.transpose(cotangent, (1, 2, 0))
    field = jax.ShapeDtypeStruct(block, F32)
    results = pl.pallas_call(
        functools.partial(kernel, sizes),
        out_shape=(field, field, field),
        in_specs=[hbm] * 9,
        out_specs=(vmem, vmem, vmem),
        scratch_shapes=[
            pltpu.VMEM((8, 8, 16), F32),
            pltpu.SMEM((2, 8), F32),
            pltpu.SMEM((16,), F32),
            pltpu.SMEM((16,), F32),
            pltpu.SMEM((3, 4), F32),
            pltpu.VMEM(block, F32),
            pltpu.VMEM(block, F32),
            pltpu.VMEM(block, F32),
            pltpu.VMEM((depth, width_x, width_y), jnp.int32),
            pltpu.VMEM((n_z, 16, 128), F32),
            pltpu.VMEM((256, n_z * 128), BF16),
            pltpu.VMEM((n_x, 288, n_z * 128), BF16),
            pltpu.VMEM((n_x, 2, half, 128), F32),
            pltpu.VMEM((n_x, 136, 128), F32),
            pltpu.VMEM((n_x - 1, 136, 128), F32),
            pltpu.VMEM((136, 128), F32),
            pltpu.VMEM((n_gz - 1, 136, 128), F32),
            pltpu.VMEM((5, half, 128), F32),
            pltpu.VMEM((8, 128), F32),
            pltpu.VMEM((8, 128), F32),
            pltpu.VMEM((8, 128), F32),
            pltpu.VMEM((8, 128), F32),
            pltpu.VMEM((2, width_x, 128), F32),
            pltpu.VMEM((8, 128), F32),
            pltpu.VMEM((8, 128), F32),
            pltpu.VMEM((8, 128), F32),
            pltpu.VMEM((8, 128), F32),
            pltpu.VMEM((2, width_x, 128), F32),
            dma((9,)),
            dma((n_z,)),
            dma((n_z,)),
            dma((n_x - 1,)),
            dma((n_x - 1,)),
            dma((1,)),
            dma((n_gz - 1,)),
            dma((6,)),
            dma((6,)),
            pltpu.SemaphoreType.REGULAR,
            pltpu.SemaphoreType.REGULAR,
        ],
        compiler_params=pltpu.CompilerParams(
            collective_id=0, has_side_effects=True, vmem_limit_bytes=60 * 1024 * 1024
        ),
    )(cot, cosines, wavenumber, time_phase, pole_table, e_field, h_field, pole_current, material)
    return tuple(
        pl.pallas_call(
            put,
            out_shape=(field, field, field),
            in_specs=[vmem] * 3,
            out_specs=(vmem,) * 3,
            compiler_params=pltpu.CompilerParams(vmem_limit_bytes=60 * 1024 * 1024),
        )(*results)
    )


def solution(mesh):
    sizes = (mesh.shape["gx"], PLANES, mesh.shape["gy"] // PLANES, mesh.shape["gz"])
    field = P(None, "gz", "gx", "gy")
    in_specs = (
        field,
        field,
        field,
        P("gz", "gx", "gy"),
        P(),
        P(None, None, ("gx", "gy", "gz")),
        P(None, ("gx", "gy", "gz")),
        P(),
        P(),
    )
    return jax.shard_map(
        functools.partial(local, sizes),
        mesh=mesh,
        in_specs=in_specs,
        out_specs=(field, field, field),
        check_vma=False,
    )
```

```python
import functools
import math

import jax
import jax.numpy as jnp
from jax import lax
from jax.experimental import pallas as pl
from jax.experimental.pallas import tpu as pltpu
from jax.sharding import PartitionSpec as P

PLANES = 4
COURANT = 0.5
MESH = pl.DeviceIdType.MESH
F32 = jnp.float32
BF16 = jnp.bfloat16

TURN = 2.0 * math.pi
TURN_HI = 6.28125
TURN_LO = TURN - TURN_HI


def sincos(phase):
    turns = jnp.floor(phase * (1.0 / TURN) + 0.5)
    rest = ((phase - turns * TURN_HI) - turns * TURN_LO) * 0.25
    sq = rest * rest
    sin = rest + rest * sq * (
        -1.6666654611e-1 + sq * (8.3321608736e-3 + sq * -1.9515295891e-4)
    )
    cos = 1.0 - 0.5 * sq + sq * sq * (
        4.166664568298827e-2 + sq * (-1.388731625493765e-3 + sq * 2.443315711809948e-5)
    )
    for _ in range(2):
        sin, cos = 2.0 * sin * cos, 1.0 - 2.0 * sin * sin
    return sin, cos


def times(a, b):
    return a[0] * b[0] - a[1] * b[1], a[0] * b[1] + a[1] * b[0]


def split(value):
    high = value.astype(BF16)
    return high, (value - high.astype(F32)).astype(BF16)


def iota(shape, dim):
    return lax.broadcasted_iota(jnp.int32, shape, dim)


def kernel(
    sizes, cot_in, cosines_in, wave_in, phase_in, table_in, e_in, h_in, p_in, m_in,
    e_out, h_out, p_out, cot, cosines, wave, phase, table, e_buf, h_buf, p_buf, m_buf,
    gat, yt, lt, cols, acc, from_x, total, from_gz, low,
    hx_out, hx_in, hy_out, hy_in, hz_in, kx_out, kx_in, ky_out, ky_in, kz_in,
    load_sem, store_sem, gat_send, gat_recv, x_send, x_recv, gz_send, gz_recv, halo_send, halo_recv,
    x_token, top_token,
):
    n_lo, n_hi, n_x, n_gz = sizes
    n_z = n_lo * n_hi
    n_half = n_z // 2
    depth, width_x, width_y = m_buf.shape
    half = width_x // 2
    gx, gy, gz = lax.axis_index("gx"), lax.axis_index("gy"), lax.axis_index("gz")
    z_hi = gy & (n_hi - 1)
    x = gy // n_hi
    def swap(k):
        return jnp.where(k < n_half, k, n_z + n_half - 1 - k)

    z = swap(z_hi * n_lo + gx)
    is_late = z >= n_half
    n_y = n_gz // 2
    y, core = gz // 2, gz & 1
    is_top = gz == n_gz - 1
    adds = core == 1

    def plane(other):
        other = swap(other)
        return {"gx": other & (n_lo - 1), "gy": x * n_hi + other // n_lo}

    def column_of(k):
        return {"gy": ((x + k) & (n_x - 1)) * n_hi + z_hi}

    def copy_to(src, dst, send_sem, recv_sem, device):
        return pltpu.make_async_remote_copy(
            src_ref=src, dst_ref=dst, send_sem=send_sem, recv_sem=recv_sem,
            device_id=device, device_id_type=MESH,
        )

    loads = [
        pltpu.make_async_copy(a, b, load_sem.at[i])
        for i, (a, b) in enumerate(
            (
                (cot_in, cot),
                (cosines_in, cosines),
                (wave_in, wave),
                (phase_in, phase),
                (e_in, e_buf),
                (h_in, h_buf),
                (p_in, p_buf),
                (m_in, m_buf),
                (table_in, table),
            )
        )
    ]
    for load in loads:
        load.start()

    wrap_low = jnp.logical_and(z_hi == n_hi - 1, x < n_x - 1)
    wrap_high = jnp.logical_and(z_hi == 0, x > 0)

    barrier = pltpu.get_barrier_semaphore()

    def greet(device):
        pl.semaphore_signal(barrier, inc=1, device_id=device, device_id_type=MESH)

    def greet_plane(other, carry):
        greet(plane(other))
        return carry

    lax.fori_loop(z + 1, n_z, greet_plane, 0)

    def greet_column(other, carry):
        greet({"gy": other * n_hi + z_hi, "gz": 2 * y + 1})

        @pl.when(adds)
        def _():
            greet({"gy": other * n_hi + z_hi, "gz": 2 * y})

        return carry

    lax.fori_loop(x + 1, n_x, greet_column, 0)

    @pl.when(gz < n_gz - 1)
    def _():
        greet({"gz": gz + 1})

    @pl.when(jnp.logical_and(adds, gz < n_gz - 1))
    def _():
        greet({"gz": n_gz - 1})

    @pl.when(wrap_high)
    def _():
        greet({"gy": gy - 1})

    @pl.when(jnp.logical_and(is_late, gx < n_lo - 1))
    def _():
        greet({"gx": gx + 1})

    @pl.when(jnp.logical_and(is_late, z_hi < n_hi - 1))
    def _():
        greet({"gy": gy + 1})

    greeted = (
        jnp.logical_and(is_late, gx > 0).astype(jnp.int32)
        + (z_hi > n_hi // 2).astype(jnp.int32)
        + z
        + x * (1 + core)
        + jnp.where(is_top, n_y, (gz > 0).astype(jnp.int32))
        + wrap_low.astype(jnp.int32)
    )

    for load in loads[:4]:
        load.wait()
    row8 = iota((8, 128), 0)
    lane8 = iota((8, 128), 1)
    lane1 = iota((1, 128), 1)
    freq = lane1 & 15
    direction = lane1 >> 4
    waves = jnp.zeros((1, 128), F32)
    delays = jnp.zeros((1, 128), F32)
    cos_x = jnp.zeros((1, 128), F32)
    cos_y = jnp.zeros((1, 128), F32)
    for f in range(16):
        waves = jnp.where(freq == f, wave[f], waves)
        delays = jnp.where(freq == f, phase[f], delays)
    for d in range(8):
        cos_x = jnp.where(direction == d, cosines[0, d], cos_x)
        cos_y = jnp.where(direction == d, cosines[1, d], cos_y)
    weights = jnp.concatenate([cot[:, d, :] for d in range(8)], axis=1)
    scale = 1.0 / math.sqrt(16.0 * 8 * n_lo * n_hi * n_x * n_gz)
    sin_t, cos_t = sincos(-delays)
    re = [weights[2 * c : 2 * c + 1] * scale for c in range(4)]
    im = [weights[2 * c + 1 : 2 * c + 2] * scale for c in range(4)]
    mine = gat.at[z]
    for c in range(4):
        mine[c : c + 1, :] = re[c] * cos_t - im[c] * sin_t
        mine[4 + c : 5 + c, :] = re[c] * sin_t + im[c] * cos_t
    mine[8:9, :] = waves * cos_x
    mine[9:10, :] = waves * cos_y

    @pl.when(greeted > 0)
    def _():
        pl.semaphore_wait(barrier, greeted)

    def share(other):
        block = gat.at[z, 0:10]
        return copy_to(block, block, gat_send.at[other], gat_recv.at[z], plane(other))

    def arrival(other):
        block = gat.at[other, 0:10]
        return copy_to(block, block, gat_send.at[other], gat_recv.at[other], plane(other))

    def share_down(other, carry):
        share(other).start()
        return carry

    lax.fori_loop(0, z, share_down, 0)

    def tell(semaphore, device):
        pl.semaphore_signal(semaphore, inc=1, device_id=device, device_id_type=MESH)

    def tell_column(other, carry):
        for which in range(2):
            tell(x_token, {"gy": other * n_hi + z_hi, "gz": 2 * y + which})
        return carry

    @pl.when(adds)
    def _():
        lax.fori_loop(0, x, tell_column, 0)
        tell(x_token, {"gz": gz - 1})

    @pl.when(is_top)
    def _():
        for k in range(n_y - 1):
            tell(top_token, {"gz": 2 * k + 1})

    loads[4].wait()
    groups = width_x // 8
    low_x, high_x = gx > 0, gx < n_lo - 1
    low_z, high_z = gz > 0, gz < n_gz - 1
    low_y, high_y = gy > 0, gy < n_hi * n_x - 1
    plain_low_y, plain_high_y = z_hi > 0, z_hi < n_hi - 1
    ex_copy = copy_to(hx_out, hx_in, halo_send.at[0], halo_recv.at[0], {"gx": gx - 1})
    ey_copy = copy_to(hy_out, hy_in, halo_send.at[1], halo_recv.at[1], {"gy": gy - 1})
    ez_copy = copy_to(
        e_buf.at[0:2, 0], hz_in, halo_send.at[2], halo_recv.at[2], {"gz": gz - 1}
    )
    hx_copy = copy_to(kx_out, kx_in, halo_send.at[3], halo_recv.at[3], {"gx": gx + 1})
    hy_copy = copy_to(ky_out, ky_in, halo_send.at[4], halo_recv.at[4], {"gy": gy + 1})
    hz_copy = copy_to(
        h_buf.at[0:2, depth - 1], kz_in, halo_send.at[5], halo_recv.at[5], {"gz": gz + 1}
    )

    def when(flag, action):
        @pl.when(flag)
        def _():
            action()

    when(low_z, ez_copy.start)
    for i in range(2):
        for j in range(depth):
            hx_out[i * depth + j : i * depth + j + 1, :] = e_buf[1 + i, j, 0:1, :]
    when(low_x, ex_copy.start)
    packed = jnp.zeros((8, 128), F32)
    for i in range(2):
        for j in range(depth):
            for g in range(groups):
                to = (i * depth + j) * groups + g
                col = e_buf[2 * i, j, 8 * g : 8 * g + 8, :]
                packed = jnp.where(lane8 == to, pltpu.roll(col, to, 1) if to else col, packed)
    hy_out[...] = packed
    when(plain_low_y, ey_copy.start)

    row = iota((width_x, 128), 0)
    lane = iota((width_x, 128), 1)

    def column(packed, which, lane_to):
        cols = []
        for g in range(groups):
            by = (lane_to - which * groups - g) % 128
            cols.append(pltpu.roll(packed, by, 1) if by else packed)
        return jnp.concatenate(cols, axis=0)

    def send_hx_hz():
        for i in range(2):
            for j in range(depth):
                kx_out[i * depth + j : i * depth + j + 1, :] = h_buf[
                    1 + i, j, width_x - 1 : width_x, :
                ]
        when(high_x, hx_copy.start)
        when(high_z, hz_copy.start)

    def magnetic():
        loads[5].wait()
        when(high_x, ex_copy.wait_recv)
        when(plain_high_y, ey_copy.wait_recv)
        when(high_z, ez_copy.wait_recv)
        x_edges = jnp.where(high_x, hx_in[...], 0.0)
        y_packed = jnp.where(plain_high_y, hy_in[...], 0.0)
        z_edges = [jnp.where(high_z, hz_in[i], 0.0) for i in range(2)]
        for j in range(depth):
            ex, ey, ez = e_buf[0, j], e_buf[1, j], e_buf[2, j]
            ex_z, ey_z = (e_buf[0, j + 1], e_buf[1, j + 1]) if j < depth - 1 else z_edges

            def up_x(v, i):
                next_row = x_edges[i * depth + j : i * depth + j + 1, :]
                return jnp.where(row == width_x - 1, next_row, pltpu.roll(v, width_x - 1, 0)) - v

            def up_y(v, i):
                next_col = column(y_packed, i * depth + j, 127)
                return jnp.where(lane == 127, next_col, pltpu.roll(v, 127, 1)) - v

            h_buf[0, j] = h_buf[0, j] - COURANT * (up_y(ez, 1) - (ey_z - ey))
            h_buf[1, j] = h_buf[1, j] - COURANT * ((ex_z - ex) - up_x(ez, 1))
            h_buf[2, j] = h_buf[2, j] - COURANT * (up_x(ey, 0) - up_y(ex, 0))

        packed = jnp.zeros((8, 128), F32)
        for i in range(2):
            for j in range(depth):
                for g in range(groups):
                    to = (i * depth + j) * groups + g
                    col = h_buf[2 * i, j, 8 * g : 8 * g + 8, :]
                    packed = jnp.where(lane8 == to, pltpu.roll(col, to + 1, 1), packed)
        ky_out[...] = packed
        when(high_y, hy_copy.start)

        when(jnp.logical_not(wrap_low), send_hx_hz)

    when(is_late, magnetic)

    rowf = row8.astype(F32)
    centre = (gx * width_x).astype(F32) + (0.5 * width_x - 0.5)
    n_a = n_x // 2
    tile_y = ((row8 * (2 * n_hi) + z_hi) * width_y).astype(F32)
    mul_x = jnp.where(
        row8 < 2, centre, jnp.where(row8 == 5, half + 0.5, jnp.where(row8 == 7, 8.0, 0.0))
    )
    mul_y = jnp.where(
        row8 < 2,
        tile_y,
        jnp.where(
            row8 == 2,
            float(n_hi * width_y),
            jnp.where(row8 == 4, 8.0, jnp.where(row8 == 6, 64.0, 0.0)),
        ),
    )
    sign = jnp.where(row8 < 4, -1.0, 1.0)

    row16 = iota((16, 128), 0)
    lane16 = iota((16, 128), 1)

    def operands(rank, s):
        along_x = gat[rank, 8:9, :]
        along_y = gat[rank, 9:10, :]
        w = gat[rank, 0:8, :]
        turned = pltpu.roll(w, 4, 0) * sign
        sin_m, cos_m = sincos(along_x * mul_x + along_y * mul_y)

        def spot(k):
            return pl.ds(pl.multiple_of(s * 256 + k * 128, 128), 128)

        sin_b, cos_b = sincos(along_y * rowf)
        run = (cos_m[2:3], sin_m[2:3])
        before_y = [(cos_b[1:2], -sin_b[1:2])]
        before_y.append(times(before_y[0], run))
        e8 = (cos_m[4:5], sin_m[4:5])
        e16 = times(e8, e8)
        more = times((cos_b, sin_b), e8)
        blocks = [(jnp.concatenate([cos_b, more[0]], 0), jnp.concatenate([sin_b, more[1]], 0))]
        for power in (e16, times(e16, e16), (cos_m[6:7], sin_m[6:7])):
            blocks = blocks + [times(b, power) for b in blocks]
        for g, block in enumerate(blocks):
            for b, moved in enumerate((block, times(block, run))):
                for kind in range(2):
                    high, lowp = split(moved[kind])
                    yt[b, 16 * g : 16 * g + 16, spot(kind)] = high
                    yt[b, 128 + 16 * g : 144 + 16 * g, spot(kind)] = lowp

        sin_b, cos_b = sincos(along_x * (rowf + 0.5))
        more = times((cos_b, sin_b), (cos_m[7:8], sin_m[7:8]))
        cx = jnp.concatenate([cos_b, more[0]], 0)
        sx = jnp.concatenate([sin_b, more[1]], 0)
        nx = -sx
        before_x = (cos_m[5:6], -sin_m[5:6])
        for t in range(n_a):
            pq = w * cos_m[t : t + 1] + turned * sin_m[t : t + 1]

            def put_left(r, k, value):
                high, lowp = split(value)
                lt[t, r : r + 16, spot(k)] = high
                lt[t, 144 + r : 160 + r, spot(k)] = lowp

            for c in range(4):
                p = pq[c : c + 1, :]
                nq = -pq[4 + c : 5 + c, :]
                products = ((p * cx, nq * cx), (nq * sx, p * nx))
                for kind in range(2):
                    for k in range(2):
                        put_left((kind * 4 + c) * half, k, products[kind][k])
                if c == 2:
                    for kind in range(2):
                        for b, edge in enumerate(before_y):
                            cols[2 * t + b, kind] = cols[2 * t + b, kind] + (
                                products[kind][0] * edge[0] + products[kind][1] * edge[1]
                            )
                if c == 3:
                    ox, oy = before_x
                    put_left(128, 0, jnp.broadcast_to(p * ox + nq * oy, (16, 128)))
                    put_left(128, 1, jnp.broadcast_to(nq * ox - p * oy, (16, 128)))

    def answer(other, carry):
        arrival(other).wait_recv()
        share(other).start()
        return carry

    def first_planes(i, carry):
        other = jnp.where(is_far, n_z - 1 - i, first_half + ((z + 1 + i) & (n_half - 1)))

        @pl.when(other != z)
        def _():
            arrival(other).wait_recv()

        @pl.when(other > z)
        def _():
            share(other).start()

        operands(other, other - first_half)
        return carry

    def second_planes(i, carry):
        other = second_half + i

        @pl.when(jnp.logical_or(other < z, is_near))
        def _():
            arrival(other).wait_recv()

        @pl.when(is_near)
        def _():
            share(other).start()

        operands(other, i)
        return carry

    def tile(t):
        both = lax.dot_general(
            lt[t // 2], yt[t & 1], (((1,), (1,)), ((), ())), preferred_element_type=F32
        )
        main = both[0:136, 0:128] + (both[0:136, 128:256] + both[144:280, 0:128])
        before = jnp.zeros((1, 128), F32)
        for kind in range(2):
            sums = jnp.sum(cols[t, kind], axis=1, keepdims=True)
            placed = jnp.where(lane16 == row16 + 16 * kind, sums, 0.0)
            before = before + jnp.sum(placed, axis=0, keepdims=True)
        cols[t] = jnp.zeros((2, 16, 128), F32)
        return main[0:128], jnp.where(row8 == 0, main[128:136], jnp.where(row8 == 1, before, 0.0))

    cols[...] = jnp.zeros(cols.shape, F32)
    is_near = z < n_half // 2
    is_far = jnp.logical_and(z >= n_half // 2, jnp.logical_not(is_late))
    first_half = jnp.where(is_near, 0, n_half)
    second_half = n_half - first_half

    @pl.when(is_far)
    def _():
        lax.fori_loop(z + 1, n_half, answer, 0)

    lax.fori_loop(0, n_half, first_planes, 0)

    def first_pass(k, carry):
        main, rest = tile((x + k) & (n_x - 1))
        acc[k, 0:128] = main
        acc[k, 128:136] = rest
        return carry

    lax.fori_loop(0, n_x, first_pass, 0)

    lax.fori_loop(0, n_half, second_planes, 0)

    def to_x(k):
        return copy_to(
            acc.at[k], from_x.at[spot_x + k], x_send.at[k], x_recv.at[spot_x + k],
            {"gy": ((x + k) & (n_x - 1)) * n_hi + z_hi, "gz": 2 * y + 1},
        )

    spot_x = jnp.where(adds, 0, n_x)
    tokens = n_x - x - core

    @pl.when(tokens > 0)
    def _():
        pl.semaphore_wait(x_token, tokens)

    def second_pass(i, carry):
        k = jnp.where(i == n_x - 1, 0, jnp.where(i == 0, n_x // 2, jnp.where(i == 1, 1, i + 1)))
        main, rest = tile((x + k) & (n_x - 1))
        acc[k, 0:128] = acc[k, 0:128] + main
        acc[k, 128:136] = acc[k, 128:136] + rest

        @pl.when(jnp.logical_or(k > 0, jnp.logical_not(adds)))
        def _():
            to_x(k).start()

        return carry

    lax.fori_loop(0, n_x, second_pass, 0)
    when(jnp.logical_not(is_late), magnetic)

    @pl.when(wrap_high)
    def _():
        hy_copy.wait_recv()
        ey_copy.start()

    @pl.when(wrap_low)
    def _():
        ey_copy.wait_recv()
        late = hy_in[...]
        for j in range(depth):
            h_buf[0, j] = h_buf[0, j] - jnp.where(
                lane == 127, COURANT * column(late, depth + j, 127), 0.0
            )
            h_buf[2, j] = h_buf[2, j] + jnp.where(
                lane == 127, COURANT * column(late, j, 127), 0.0
            )
        send_hx_hz()

    def to_top(k):
        return copy_to(
            total, from_gz.at[k], gz_send.at[0], gz_recv.at[k], {"gz": n_gz - 1}
        )

    @pl.when(adds)
    def _():
        for k in range(1, 2 * n_x):
            copy_to(
                acc.at[0], from_x.at[k], x_send.at[0], x_recv.at[k], {"gz": 2 * y}
            ).wait_recv()
        total[...] = sum((from_x[k] for k in range(1, 2 * n_x)), acc[0])

    sends_up = jnp.logical_and(adds, jnp.logical_not(is_top))

    @pl.when(sends_up)
    def _():
        pl.semaphore_wait(top_token, 1)
        to_top(y).start()

    for load in loads[6:]:
        load.wait()
    when(low_x, hx_copy.wait_recv)
    when(plain_low_y, hy_copy.wait_recv)
    when(low_z, hz_copy.wait_recv)
    x_edges = jnp.where(low_x, kx_in[...], 0.0)
    y_packed = jnp.where(low_y, ky_in[...], 0.0)
    z_edges = [jnp.where(low_z, kz_in[i], 0.0) for i in range(2)]
    missing = jnp.where(wrap_high, COURANT, 0.0)
    when(low_z, ez_copy.wait_send)

    def chosen(which, m):
        value = jnp.full(m.shape, table[which, 3], F32)
        for i in range(3):
            value = jnp.where(m == i, table[which, i], value)
        return value

    for j in range(depth):
        hx, hy, hz = h_buf[0, j], h_buf[1, j], h_buf[2, j]
        hx_z, hy_z = (h_buf[0, j - 1], h_buf[1, j - 1]) if j > 0 else z_edges
        ex, ey, ez = e_buf[0, j], e_buf[1, j], e_buf[2, j]

        def down_x(v, i):
            last_row = x_edges[i * depth + j : i * depth + j + 1, :]
            return v - jnp.where(row == 0, last_row, pltpu.roll(v, 1, 0))

        def down_y(v, i, rest):
            last_col = column(y_packed, i * depth + j, 0) + rest
            return v - jnp.where(lane == 0, last_col, pltpu.roll(v, 1, 1))

        side = (
            down_y(hz, 1, missing * ex) - (hy - hy_z),
            (hx - hx_z) - down_x(hz, 1),
            down_x(hy, 0) - down_y(hx, 0, -missing * ez),
        )
        m = m_buf[j]
        decay, drive, coef = chosen(0, m), chosen(1, m), chosen(2, m)
        for i, e in enumerate((ex, ey, ez)):
            pole = p_buf[i, j]
            after = decay * pole + drive * e
            p_buf[i, j] = after
            e_buf[i, j] = e + coef * (side[i] - 0.5 * (after + pole))

    last = depth - 1
    stores = [
        pltpu.make_async_copy(a, b, store_sem.at[k])
        for k, (a, b) in enumerate(
            (
                (p_buf, p_out),
                (h_buf.at[:, 0:last], h_out.at[:, 0:last]),
                (e_buf.at[:, 0:last], e_out.at[:, 0:last]),
                (h_buf.at[:, last], h_out.at[:, last]),
                (e_buf.at[:, last], e_out.at[:, last]),
            )
        )
    ]
    for store in stores[:3]:
        store.start()

    @pl.when(is_top)
    def _():
        for k in range(n_y - 1):
            copy_to(
                total, from_gz.at[k], gz_send.at[0], gz_recv.at[k], {"gz": 0}
            ).wait_recv()
        summed = sum((from_gz[k] for k in range(n_y - 1)), total[...])

        def unfold(even, odd, spot):
            lower = even - odd
            for j in range(half):
                low[spot, half - 1 - j : half - j, :] = lower[j : j + 1, :]
            return jnp.concatenate([low[spot], even + odd], axis=0)

        src = [
            unfold(
                summed[c * half : (c + 1) * half], summed[(4 + c) * half : (5 + c) * half], c
            )
            for c in range(4)
        ]
        near_x = jnp.where(low_x, summed[128:129], 0.0)
        before = jnp.where(low_y, summed[129:130], 0.0)
        sides = [
            jnp.broadcast_to(
                jnp.sum(
                    jnp.where(lane16 == row16 + 16 * kind, before, 0.0), axis=1, keepdims=True
                ),
                (16, 128),
            )
            for kind in range(2)
        ]
        near_y = unfold(sides[0], sides[1], 4)
        coef = chosen(2, m_buf[last])
        h_buf[0, last] = h_buf[0, last] - COURANT * src[2]
        h_buf[1, last] = h_buf[1, last] - COURANT * src[3]
        behind_x = src[3] - jnp.where(row == 0, near_x, pltpu.roll(src[3], 1, 0))
        behind_y = src[2] - jnp.where(lane == 0, near_y, pltpu.roll(src[2], 1, 1))
        e_buf[0, last] = e_buf[0, last] + coef * (COURANT * src[3] - src[0])
        e_buf[1, last] = e_buf[1, last] - coef * (COURANT * src[2] + src[1])
        e_buf[2, last] = e_buf[2, last] - coef * (COURANT * (behind_x - behind_y))

    for store in stores[3:]:
        store.start()
    for store in stores:
        store.wait()

    def sent(other, carry):
        @pl.when(other != z)
        def _():
            share(other).wait_send()

        return carry

    lax.fori_loop(0, n_z, sent, 0)
    for k in range(1, n_x):
        to_x(k).wait_send()
    when(jnp.logical_not(adds), to_x(0).wait_send)
    when(low_x, ex_copy.wait_send)
    when(low_y, ey_copy.wait_send)
    when(high_x, hx_copy.wait_send)
    when(high_y, hy_copy.wait_send)
    when(high_z, hz_copy.wait_send)
    when(sends_up, to_top(y).wait_send)


def put(*refs):
    for src, dst in zip(refs[:3], refs[3:]):
        dst[...] = src[...]


def local(
    sizes, e_field, h_field, pole_current, material, pole_table, cotangent, cosines, wavenumber,
    time_phase,
):
    n_lo, n_hi, n_x, n_gz = sizes
    n_z = n_lo * n_hi
    depth, width_x, width_y = material.shape
    half = width_x // 2
    block = (3, depth, width_x, width_y)
    vmem = pl.BlockSpec(memory_space=pltpu.VMEM)
    hbm = pl.BlockSpec(memory_space=pl.ANY)
    dma = pltpu.SemaphoreType.DMA
    cot = jnp.transpose(cotangent, (1, 2, 0))
    field = jax.ShapeDtypeStruct(block, F32)
    results = pl.pallas_call(
        functools.partial(kernel, sizes),
        out_shape=(field, field, field),
        in_specs=[hbm] * 9,
        out_specs=(hbm, hbm, hbm),
        scratch_shapes=[
            pltpu.VMEM((8, 8, 16), F32),
            pltpu.SMEM((2, 8), F32),
            pltpu.SMEM((16,), F32),
            pltpu.SMEM((16,), F32),
            pltpu.SMEM((3, 4), F32),
            pltpu.VMEM(block, F32),
            pltpu.VMEM(block, F32),
            pltpu.VMEM(block, F32),
            pltpu.VMEM((depth, width_x, width_y), jnp.int32),
            pltpu.VMEM((n_z, 16, 128), F32),
            pltpu.VMEM((2, 256, n_z * 128), BF16),
            pltpu.VMEM((n_x // 2, 288, n_z * 128), BF16),
            pltpu.VMEM((n_x, 2, half, 128), F32),
            pltpu.VMEM((n_x, 136, 128), F32),
            pltpu.VMEM((2 * n_x, 136, 128), F32),
            pltpu.VMEM((136, 128), F32),
            pltpu.VMEM((max(n_gz // 2 - 1, 1), 136, 128), F32),
            pltpu.VMEM((5, half, 128), F32),
            pltpu.VMEM((8, 128), F32),
            pltpu.VMEM((8, 128), F32),
            pltpu.VMEM((8, 128), F32),
            pltpu.VMEM((8, 128), F32),
            pltpu.VMEM((2, width_x, 128), F32),
            pltpu.VMEM((8, 128), F32),
            pltpu.VMEM((8, 128), F32),
            pltpu.VMEM((8, 128), F32),
            pltpu.VMEM((8, 128), F32),
            pltpu.VMEM((2, width_x, 128), F32),
            dma((9,)),
            dma((5,)),
            dma((n_z,)),
            dma((n_z,)),
            dma((n_x,)),
            dma((2 * n_x,)),
            dma((1,)),
            dma((max(n_gz // 2 - 1, 1),)),
            dma((6,)),
            dma((6,)),
            pltpu.SemaphoreType.REGULAR,
            pltpu.SemaphoreType.REGULAR,
        ],
        compiler_params=pltpu.CompilerParams(
            collective_id=0, has_side_effects=True, vmem_limit_bytes=60 * 1024 * 1024
        ),
    )(cot, cosines, wavenumber, time_phase, pole_table, e_field, h_field, pole_current, material)
    return tuple(
        pl.pallas_call(
            put,
            out_shape=(field, field, field),
            in_specs=[vmem] * 3,
            out_specs=(vmem,) * 3,
            compiler_params=pltpu.CompilerParams(vmem_limit_bytes=60 * 1024 * 1024),
        )(*results)
    )


def solution(mesh):
    sizes = (mesh.shape["gx"], PLANES, mesh.shape["gy"] // PLANES, mesh.shape["gz"])
    field = P(None, "gz", "gx", "gy")
    in_specs = (
        field,
        field,
        field,
        P("gz", "gx", "gy"),
        P(),
        P(None, None, ("gx", "gy", "gz")),
        P(None, ("gx", "gy", "gz")),
        P(),
        P(),
    )
    return jax.shard_map(
        functools.partial(local, sizes),
        mesh=mesh,
        in_specs=in_specs,
        out_specs=(field, field, field),
        check_vma=False,
    )
```

```python
import functools
import math

import jax
import jax.numpy as jnp
from jax import lax
from jax.experimental import pallas as pl
from jax.experimental.pallas import tpu as pltpu
from jax.sharding import PartitionSpec as P

PLANES = 4
COURANT = 0.5
MESH = pl.DeviceIdType.MESH
F32 = jnp.float32
BF16 = jnp.bfloat16

TURN = 2.0 * math.pi
TURN_HI = 6.28125
TURN_LO = TURN - TURN_HI


def sincos(phase):
    turns = jnp.floor(phase * (1.0 / TURN) + 0.5)
    rest = ((phase - turns * TURN_HI) - turns * TURN_LO) * 0.25
    sq = rest * rest
    sin = rest + rest * sq * (
        -1.6666654611e-1 + sq * (8.3321608736e-3 + sq * -1.9515295891e-4)
    )
    cos = 1.0 - 0.5 * sq + sq * sq * (
        4.166664568298827e-2 + sq * (-1.388731625493765e-3 + sq * 2.443315711809948e-5)
    )
    for _ in range(2):
        sin, cos = 2.0 * sin * cos, 1.0 - 2.0 * sin * sin
    return sin, cos


def times(a, b):
    return a[0] * b[0] - a[1] * b[1], a[0] * b[1] + a[1] * b[0]


def split(value):
    high = value.astype(BF16)
    return high, (value - high.astype(F32)).astype(BF16)


def iota(shape, dim):
    return lax.broadcasted_iota(jnp.int32, shape, dim)


def kernel(
    sizes, cot_in, cosines_in, wave_in, phase_in, table_in, e_in, h_in, p_in, m_in,
    e_out, h_out, p_out, cot, cosines, wave, phase, table, e_buf, h_buf, p_buf, m_buf,
    gat, yt, lt, cols, acc, from_x, total, from_gz, low,
    hx_out, hx_in, hy_out, hy_in, hz_in, kx_out, kx_in, ky_out, ky_in, kz_in,
    load_sem, store_sem, gat_send, gat_recv, x_send, x_recv, gz_send, gz_recv, halo_send, halo_recv,
    x_token, top_token,
):
    n_lo, n_hi, n_x, n_gz = sizes
    n_z = n_lo * n_hi
    n_half = n_z // 2
    depth, width_x, width_y = m_buf.shape
    half = width_x // 2
    gx, gy, gz = lax.axis_index("gx"), lax.axis_index("gy"), lax.axis_index("gz")
    z_hi = gy & (n_hi - 1)
    x = gy // n_hi
    def swap(k):
        return jnp.where(k < n_half, k, n_z + n_half - 1 - k)

    z = swap(z_hi * n_lo + gx)
    is_late = z >= n_half
    n_y = n_gz // 2
    y, core = gz // 2, gz & 1
    is_top = gz == n_gz - 1
    adds = core == 1

    def plane(other):
        other = swap(other)
        return {"gx": other & (n_lo - 1), "gy": x * n_hi + other // n_lo}

    def column_of(k):
        return {"gy": ((x + k) & (n_x - 1)) * n_hi + z_hi}

    def copy_to(src, dst, send_sem, recv_sem, device):
        return pltpu.make_async_remote_copy(
            src_ref=src, dst_ref=dst, send_sem=send_sem, recv_sem=recv_sem,
            device_id=device, device_id_type=MESH,
        )

    loads = [
        pltpu.make_async_copy(a, b, load_sem.at[i])
        for i, (a, b) in enumerate(
            (
                (cot_in, cot),
                (cosines_in, cosines),
                (wave_in, wave),
                (phase_in, phase),
                (e_in, e_buf),
                (h_in, h_buf),
                (p_in, p_buf),
                (m_in, m_buf),
                (table_in, table),
            )
        )
    ]
    for load in loads[:4]:
        load.start()

    wrap_low = jnp.logical_and(z_hi == n_hi - 1, x < n_x - 1)
    wrap_high = jnp.logical_and(z_hi == 0, x > 0)

    barrier = pltpu.get_barrier_semaphore()

    def greet(device):
        pl.semaphore_signal(barrier, inc=1, device_id=device, device_id_type=MESH)

    def greet_plane(i, carry):
        greet(plane(n_z - 1 - i))
        return carry

    lax.fori_loop(0, n_z - 1 - z, greet_plane, 0)

    def greet_column(other, carry):
        greet({"gy": other * n_hi + z_hi, "gz": 2 * y + 1})

        @pl.when(adds)
        def _():
            greet({"gy": other * n_hi + z_hi, "gz": 2 * y})

        return carry

    lax.fori_loop(x + 1, n_x, greet_column, 0)

    @pl.when(gz < n_gz - 1)
    def _():
        greet({"gz": gz + 1})

    @pl.when(jnp.logical_and(adds, gz < n_gz - 1))
    def _():
        greet({"gz": n_gz - 1})

    @pl.when(wrap_high)
    def _():
        greet({"gy": gy - 1})

    @pl.when(jnp.logical_and(is_late, gx < n_lo - 1))
    def _():
        greet({"gx": gx + 1})

    @pl.when(jnp.logical_and(is_late, z_hi < n_hi - 1))
    def _():
        greet({"gy": gy + 1})

    greeted = (
        jnp.logical_and(is_late, gx > 0).astype(jnp.int32)
        + (z_hi > n_hi // 2).astype(jnp.int32)
        + z
        + x * (1 + core)
        + jnp.where(is_top, n_y, (gz > 0).astype(jnp.int32))
        + wrap_low.astype(jnp.int32)
    )

    for load in loads[4:]:
        load.start()
    for load in loads[:4]:
        load.wait()
    row8 = iota((8, 128), 0)
    lane8 = iota((8, 128), 1)
    lane1 = iota((1, 128), 1)
    freq = lane1 & 15
    direction = lane1 >> 4
    waves = jnp.zeros((1, 128), F32)
    delays = jnp.zeros((1, 128), F32)
    cos_x = jnp.zeros((1, 128), F32)
    cos_y = jnp.zeros((1, 128), F32)
    for f in range(16):
        waves = jnp.where(freq == f, wave[f], waves)
        delays = jnp.where(freq == f, phase[f], delays)
    for d in range(8):
        cos_x = jnp.where(direction == d, cosines[0, d], cos_x)
        cos_y = jnp.where(direction == d, cosines[1, d], cos_y)
    weights = jnp.concatenate([cot[:, d, :] for d in range(8)], axis=1)
    scale = 1.0 / math.sqrt(16.0 * 8 * n_lo * n_hi * n_x * n_gz)
    sin_t, cos_t = sincos(-delays)
    re = [weights[2 * c : 2 * c + 1] * scale for c in range(4)]
    im = [weights[2 * c + 1 : 2 * c + 2] * scale for c in range(4)]
    mine = gat.at[z]
    for c in range(4):
        mine[c : c + 1, :] = re[c] * cos_t - im[c] * sin_t
        mine[4 + c : 5 + c, :] = re[c] * sin_t + im[c] * cos_t
    mine[8:9, :] = waves * cos_x
    mine[9:10, :] = waves * cos_y

    @pl.when(greeted > 0)
    def _():
        pl.semaphore_wait(barrier, greeted)

    def share(other):
        block = gat.at[z, 0:10]
        return copy_to(block, block, gat_send.at[other], gat_recv.at[z], plane(other))

    def arrival(other):
        block = gat.at[other, 0:10]
        return copy_to(block, block, gat_send.at[other], gat_recv.at[other], plane(other))

    def share_down(other, carry):
        share(other).start()
        return carry

    lax.fori_loop(0, z, share_down, 0)

    def tell(semaphore, device):
        pl.semaphore_signal(semaphore, inc=1, device_id=device, device_id_type=MESH)

    def tell_column(other, carry):
        for which in range(2):
            tell(x_token, {"gy": other * n_hi + z_hi, "gz": 2 * y + which})
        return carry

    @pl.when(adds)
    def _():
        lax.fori_loop(0, x, tell_column, 0)
        tell(x_token, {"gz": gz - 1})

    @pl.when(is_top)
    def _():
        for k in range(n_y - 1):
            tell(top_token, {"gz": 2 * k + 1})

    loads[4].wait()
    groups = width_x // 8
    low_x, high_x = gx > 0, gx < n_lo - 1
    low_z, high_z = gz > 0, gz < n_gz - 1
    low_y, high_y = gy > 0, gy < n_hi * n_x - 1
    plain_low_y, plain_high_y = z_hi > 0, z_hi < n_hi - 1
    ex_copy = copy_to(hx_out, hx_in, halo_send.at[0], halo_recv.at[0], {"gx": gx - 1})
    ey_copy = copy_to(hy_out, hy_in, halo_send.at[1], halo_recv.at[1], {"gy": gy - 1})
    ez_copy = copy_to(
        e_buf.at[0:2, 0], hz_in, halo_send.at[2], halo_recv.at[2], {"gz": gz - 1}
    )
    hx_copy = copy_to(kx_out, kx_in, halo_send.at[3], halo_recv.at[3], {"gx": gx + 1})
    hy_copy = copy_to(ky_out, ky_in, halo_send.at[4], halo_recv.at[4], {"gy": gy + 1})
    hz_copy = copy_to(
        h_buf.at[0:2, depth - 1], kz_in, halo_send.at[5], halo_recv.at[5], {"gz": gz + 1}
    )

    def when(flag, action):
        @pl.when(flag)
        def _():
            action()

    when(low_z, ez_copy.start)
    for i in range(2):
        for j in range(depth):
            hx_out[i * depth + j : i * depth + j + 1, :] = e_buf[1 + i, j, 0:1, :]
    when(low_x, ex_copy.start)
    packed = jnp.zeros((8, 128), F32)
    for i in range(2):
        for j in range(depth):
            for g in range(groups):
                to = (i * depth + j) * groups + g
                col = e_buf[2 * i, j, 8 * g : 8 * g + 8, :]
                packed = jnp.where(lane8 == to, pltpu.roll(col, to, 1) if to else col, packed)
    hy_out[...] = packed
    when(plain_low_y, ey_copy.start)

    row = iota((width_x, 128), 0)
    lane = iota((width_x, 128), 1)

    def column(packed, which, lane_to):
        cols = []
        for g in range(groups):
            by = (lane_to - which * groups - g) % 128
            cols.append(pltpu.roll(packed, by, 1) if by else packed)
        return jnp.concatenate(cols, axis=0)

    def send_hx_hz():
        for i in range(2):
            for j in range(depth):
                kx_out[i * depth + j : i * depth + j + 1, :] = h_buf[
                    1 + i, j, width_x - 1 : width_x, :
                ]
        when(high_x, hx_copy.start)
        when(high_z, hz_copy.start)

    def magnetic():
        loads[5].wait()
        when(high_x, ex_copy.wait_recv)
        when(plain_high_y, ey_copy.wait_recv)
        when(high_z, ez_copy.wait_recv)
        x_edges = jnp.where(high_x, hx_in[...], 0.0)
        y_packed = jnp.where(plain_high_y, hy_in[...], 0.0)
        z_edges = [jnp.where(high_z, hz_in[i], 0.0) for i in range(2)]
        for j in range(depth):
            ex, ey, ez = e_buf[0, j], e_buf[1, j], e_buf[2, j]
            ex_z, ey_z = (e_buf[0, j + 1], e_buf[1, j + 1]) if j < depth - 1 else z_edges

            def up_x(v, i):
                next_row = x_edges[i * depth + j : i * depth + j + 1, :]
                return jnp.where(row == width_x - 1, next_row, pltpu.roll(v, width_x - 1, 0)) - v

            def up_y(v, i):
                next_col = column(y_packed, i * depth + j, 127)
                return jnp.where(lane == 127, next_col, pltpu.roll(v, 127, 1)) - v

            h_buf[0, j] = h_buf[0, j] - COURANT * (up_y(ez, 1) - (ey_z - ey))
            h_buf[1, j] = h_buf[1, j] - COURANT * ((ex_z - ex) - up_x(ez, 1))
            h_buf[2, j] = h_buf[2, j] - COURANT * (up_x(ey, 0) - up_y(ex, 0))

        packed = jnp.zeros((8, 128), F32)
        for i in range(2):
            for j in range(depth):
                for g in range(groups):
                    to = (i * depth + j) * groups + g
                    col = h_buf[2 * i, j, 8 * g : 8 * g + 8, :]
                    packed = jnp.where(lane8 == to, pltpu.roll(col, to + 1, 1), packed)
        ky_out[...] = packed
        when(high_y, hy_copy.start)

        when(jnp.logical_not(wrap_low), send_hx_hz)

    when(is_late, magnetic)

    rowf = row8.astype(F32)
    centre = (gx * width_x).astype(F32) + (0.5 * width_x - 0.5)
    n_a = n_x // 2
    tile_y = ((row8 * (2 * n_hi) + z_hi) * width_y).astype(F32)
    mul_x = jnp.where(
        row8 < 2, centre, jnp.where(row8 == 5, half + 0.5, jnp.where(row8 == 7, 8.0, 0.0))
    )
    mul_y = jnp.where(
        row8 < 2,
        tile_y,
        jnp.where(
            row8 == 2,
            float(n_hi * width_y),
            jnp.where(row8 == 4, 8.0, jnp.where(row8 == 6, 64.0, 0.0)),
        ),
    )
    sign = jnp.where(row8 < 4, -1.0, 1.0)

    row16 = iota((16, 128), 0)
    lane16 = iota((16, 128), 1)

    def operands(rank, s):
        along_x = gat[rank, 8:9, :]
        along_y = gat[rank, 9:10, :]
        w = gat[rank, 0:8, :]
        turned = pltpu.roll(w, 4, 0) * sign
        sin_m, cos_m = sincos(along_x * mul_x + along_y * mul_y)

        def spot(k):
            return pl.ds(pl.multiple_of(s * 256 + k * 128, 128), 128)

        sin_b, cos_b = sincos(along_y * rowf)
        run = (cos_m[2:3], sin_m[2:3])
        before_y = [(cos_b[1:2], -sin_b[1:2])]
        before_y.append(times(before_y[0], run))
        e8 = (cos_m[4:5], sin_m[4:5])
        e16 = times(e8, e8)
        more = times((cos_b, sin_b), e8)
        blocks = [(jnp.concatenate([cos_b, more[0]], 0), jnp.concatenate([sin_b, more[1]], 0))]
        for power in (e16, times(e16, e16), (cos_m[6:7], sin_m[6:7])):
            blocks = blocks + [times(b, power) for b in blocks]
        for g, block in enumerate(blocks):
            for b, moved in enumerate((block, times(block, run))):
                for kind in range(2):
                    high, lowp = split(moved[kind])
                    yt[b, 16 * g : 16 * g + 16, spot(kind)] = high
                    yt[b, 128 + 16 * g : 144 + 16 * g, spot(kind)] = lowp

        sin_b, cos_b = sincos(along_x * (rowf + 0.5))
        more = times((cos_b, sin_b), (cos_m[7:8], sin_m[7:8]))
        cx = jnp.concatenate([cos_b, more[0]], 0)
        sx = jnp.concatenate([sin_b, more[1]], 0)
        nx = -sx
        before_x = (cos_m[5:6], -sin_m[5:6])
        for t in range(n_a):
            pq = w * cos_m[t : t + 1] + turned * sin_m[t : t + 1]

            def put_left(r, k, value):
                high, lowp = split(value)
                lt[t, r : r + 16, spot(k)] = high
                lt[t, 144 + r : 160 + r, spot(k)] = lowp

            for c in range(4):
                p = pq[c : c + 1, :]
                nq = -pq[4 + c : 5 + c, :]
                products = ((p * cx, nq * cx), (nq * sx, p * nx))
                for kind in range(2):
                    for k in range(2):
                        put_left((kind * 4 + c) * half, k, products[kind][k])
                if c == 2:
                    for kind in range(2):
                        for b, edge in enumerate(before_y):
                            cols[2 * t + b, kind] = cols[2 * t + b, kind] + (
                                products[kind][0] * edge[0] + products[kind][1] * edge[1]
                            )
                if c == 3:
                    ox, oy = before_x
                    put_left(128, 0, jnp.broadcast_to(p * ox + nq * oy, (16, 128)))
                    put_left(128, 1, jnp.broadcast_to(nq * ox - p * oy, (16, 128)))

    def answer(other, carry):
        arrival(other).wait_recv()
        share(other).start()
        return carry

    def first_planes(i, carry):
        other = jnp.where(is_far, n_z - 1 - i, first_half + ((z + 1 + i) & (n_half - 1)))

        @pl.when(other != z)
        def _():
            arrival(other).wait_recv()

        @pl.when(other > z)
        def _():
            share(other).start()

        operands(other, other - first_half)
        return carry

    def second_planes(i, carry):
        other = second_half + i

        @pl.when(jnp.logical_or(other < z, is_near))
        def _():
            arrival(other).wait_recv()

        @pl.when(is_near)
        def _():
            share(other).start()

        operands(other, i)
        return carry

    def tile(t):
        both = lax.dot_general(
            lt[t // 2], yt[t & 1], (((1,), (1,)), ((), ())), preferred_element_type=F32
        )
        main = both[0:136, 0:128] + (both[0:136, 128:256] + both[144:280, 0:128])
        before = jnp.zeros((1, 128), F32)
        for kind in range(2):
            sums = jnp.sum(cols[t, kind], axis=1, keepdims=True)
            placed = jnp.where(lane16 == row16 + 16 * kind, sums, 0.0)
            before = before + jnp.sum(placed, axis=0, keepdims=True)
        cols[t] = jnp.zeros((2, 16, 128), F32)
        return main[0:128], jnp.where(row8 == 0, main[128:136], jnp.where(row8 == 1, before, 0.0))

    cols[...] = jnp.zeros(cols.shape, F32)
    is_near = z < n_half // 2
    is_far = jnp.logical_and(z >= n_half // 2, jnp.logical_not(is_late))
    first_half = jnp.where(is_near, 0, n_half)
    second_half = n_half - first_half

    @pl.when(is_far)
    def _():
        lax.fori_loop(z + 1, n_half, answer, 0)

    lax.fori_loop(0, n_half, first_planes, 0)

    def first_pass(k, carry):
        main, rest = tile((x + k) & (n_x - 1))
        acc[k, 0:128] = main
        acc[k, 128:136] = rest
        return carry

    lax.fori_loop(0, n_x, first_pass, 0)

    lax.fori_loop(0, n_half, second_planes, 0)

    def to_x(k):
        return copy_to(
            acc.at[k], from_x.at[spot_x + k], x_send.at[k], x_recv.at[spot_x + k],
            {"gy": ((x + k) & (n_x - 1)) * n_hi + z_hi, "gz": 2 * y + 1},
        )

    spot_x = jnp.where(adds, 0, n_x)
    tokens = n_x - x - core

    @pl.when(tokens > 0)
    def _():
        pl.semaphore_wait(x_token, tokens)

    def second_pass(i, carry):
        k = jnp.where(i == n_x - 1, 0, jnp.where(i == 0, n_x // 2, jnp.where(i == 1, 1, i + 1)))
        main, rest = tile((x + k) & (n_x - 1))
        acc[k, 0:128] = acc[k, 0:128] + main
        acc[k, 128:136] = acc[k, 128:136] + rest

        @pl.when(jnp.logical_or(k > 0, jnp.logical_not(adds)))
        def _():
            to_x(k).start()

        return carry

    lax.fori_loop(0, n_x, second_pass, 0)
    when(jnp.logical_not(is_late), magnetic)

    @pl.when(wrap_high)
    def _():
        hy_copy.wait_recv()
        ey_copy.start()

    @pl.when(wrap_low)
    def _():
        ey_copy.wait_recv()
        late = hy_in[...]
        for j in range(depth):
            h_buf[0, j] = h_buf[0, j] - jnp.where(
                lane == 127, COURANT * column(late, depth + j, 127), 0.0
            )
            h_buf[2, j] = h_buf[2, j] + jnp.where(
                lane == 127, COURANT * column(late, j, 127), 0.0
            )
        send_hx_hz()

    def to_top(k):
        return copy_to(
            total, from_gz.at[k], gz_send.at[0], gz_recv.at[k], {"gz": n_gz - 1}
        )

    @pl.when(adds)
    def _():
        for k in range(1, 2 * n_x):
            copy_to(
                acc.at[0], from_x.at[k], x_send.at[0], x_recv.at[k], {"gz": 2 * y}
            ).wait_recv()
        total[...] = sum((from_x[k] for k in range(1, 2 * n_x)), acc[0])

    sends_up = jnp.logical_and(adds, jnp.logical_not(is_top))

    @pl.when(sends_up)
    def _():
        pl.semaphore_wait(top_token, 1)
        to_top(y).start()

    for load in loads[6:]:
        load.wait()
    when(low_x, hx_copy.wait_recv)
    when(plain_low_y, hy_copy.wait_recv)
    when(low_z, hz_copy.wait_recv)
    x_edges = jnp.where(low_x, kx_in[...], 0.0)
    y_packed = jnp.where(low_y, ky_in[...], 0.0)
    z_edges = [jnp.where(low_z, kz_in[i], 0.0) for i in range(2)]
    missing = jnp.where(wrap_high, COURANT, 0.0)
    when(low_z, ez_copy.wait_send)

    def chosen(which, m):
        value = jnp.full(m.shape, table[which, 3], F32)
        for i in range(3):
            value = jnp.where(m == i, table[which, i], value)
        return value

    for j in range(depth):
        hx, hy, hz = h_buf[0, j], h_buf[1, j], h_buf[2, j]
        hx_z, hy_z = (h_buf[0, j - 1], h_buf[1, j - 1]) if j > 0 else z_edges
        ex, ey, ez = e_buf[0, j], e_buf[1, j], e_buf[2, j]

        def down_x(v, i):
            last_row = x_edges[i * depth + j : i * depth + j + 1, :]
            return v - jnp.where(row == 0, last_row, pltpu.roll(v, 1, 0))

        def down_y(v, i, rest):
            last_col = column(y_packed, i * depth + j, 0) + rest
            return v - jnp.where(lane == 0, last_col, pltpu.roll(v, 1, 1))

        side = (
            down_y(hz, 1, missing * ex) - (hy - hy_z),
            (hx - hx_z) - down_x(hz, 1),
            down_x(hy, 0) - down_y(hx, 0, -missing * ez),
        )
        m = m_buf[j]
        decay, drive, coef = chosen(0, m), chosen(1, m), chosen(2, m)
        for i, e in enumerate((ex, ey, ez)):
            pole = p_buf[i, j]
            after = decay * pole + drive * e
            p_buf[i, j] = after
            e_buf[i, j] = e + coef * (side[i] - 0.5 * (after + pole))

    last = depth - 1
    stores = [
        pltpu.make_async_copy(a, b, store_sem.at[k])
        for k, (a, b) in enumerate(
            (
                (p_buf, p_out),
                (h_buf.at[:, 0:last], h_out.at[:, 0:last]),
                (e_buf.at[:, 0:last], e_out.at[:, 0:last]),
                (h_buf.at[:, last], h_out.at[:, last]),
                (e_buf.at[:, last], e_out.at[:, last]),
            )
        )
    ]
    for store in stores[:3]:
        store.start()

    def sent(other, carry):
        @pl.when(other != z)
        def _():
            share(other).wait_send()

        return carry

    lax.fori_loop(0, n_z, sent, 0)
    for k in range(1, n_x):
        to_x(k).wait_send()
    when(jnp.logical_not(adds), to_x(0).wait_send)
    when(low_x, ex_copy.wait_send)
    when(low_y, ey_copy.wait_send)
    when(high_x, hx_copy.wait_send)
    when(high_y, hy_copy.wait_send)
    when(high_z, hz_copy.wait_send)

    @pl.when(is_top)
    def _():
        for k in range(n_y - 1):
            copy_to(
                total, from_gz.at[k], gz_send.at[0], gz_recv.at[k], {"gz": 0}
            ).wait_recv()
        summed = sum((from_gz[k] for k in range(n_y - 1)), total[...])

        def unfold(even, odd, spot):
            lower = even - odd
            for j in range(half):
                low[spot, half - 1 - j : half - j, :] = lower[j : j + 1, :]
            return jnp.concatenate([low[spot], even + odd], axis=0)

        src = [
            unfold(
                summed[c * half : (c + 1) * half], summed[(4 + c) * half : (5 + c) * half], c
            )
            for c in range(4)
        ]
        near_x = jnp.where(low_x, summed[128:129], 0.0)
        before = jnp.where(low_y, summed[129:130], 0.0)
        sides = [
            jnp.broadcast_to(
                jnp.sum(
                    jnp.where(lane16 == row16 + 16 * kind, before, 0.0), axis=1, keepdims=True
                ),
                (16, 128),
            )
            for kind in range(2)
        ]
        near_y = unfold(sides[0], sides[1], 4)
        coef = chosen(2, m_buf[last])
        h_buf[0, last] = h_buf[0, last] - COURANT * src[2]
        h_buf[1, last] = h_buf[1, last] - COURANT * src[3]
        behind_x = src[3] - jnp.where(row == 0, near_x, pltpu.roll(src[3], 1, 0))
        behind_y = src[2] - jnp.where(lane == 0, near_y, pltpu.roll(src[2], 1, 1))
        e_buf[0, last] = e_buf[0, last] + coef * (COURANT * src[3] - src[0])
        e_buf[1, last] = e_buf[1, last] - coef * (COURANT * src[2] + src[1])
        e_buf[2, last] = e_buf[2, last] - coef * (COURANT * (behind_x - behind_y))

    for store in stores[3:]:
        store.start()
    for store in stores:
        store.wait()

    when(sends_up, to_top(y).wait_send)


def put(*refs):
    for src, dst in zip(refs[:3], refs[3:]):
        dst[...] = src[...]


def local(
    sizes, e_field, h_field, pole_current, material, pole_table, cotangent, cosines, wavenumber,
    time_phase,
):
    n_lo, n_hi, n_x, n_gz = sizes
    n_z = n_lo * n_hi
    depth, width_x, width_y = material.shape
    half = width_x // 2
    block = (3, depth, width_x, width_y)
    vmem = pl.BlockSpec(memory_space=pltpu.VMEM)
    hbm = pl.BlockSpec(memory_space=pl.ANY)
    dma = pltpu.SemaphoreType.DMA
    cot = jnp.transpose(cotangent, (1, 2, 0))
    field = jax.ShapeDtypeStruct(block, F32)
    results = pl.pallas_call(
        functools.partial(kernel, sizes),
        out_shape=(field, field, field),
        in_specs=[hbm] * 9,
        out_specs=(hbm, hbm, hbm),
        scratch_shapes=[
            pltpu.VMEM((8, 8, 16), F32),
            pltpu.SMEM((2, 8), F32),
            pltpu.SMEM((16,), F32),
            pltpu.SMEM((16,), F32),
            pltpu.SMEM((3, 4), F32),
            pltpu.VMEM(block, F32),
            pltpu.VMEM(block, F32),
            pltpu.VMEM(block, F32),
            pltpu.VMEM((depth, width_x, width_y), jnp.int32),
            pltpu.VMEM((n_z, 16, 128), F32),
            pltpu.VMEM((2, 256, n_z * 128), BF16),
            pltpu.VMEM((n_x // 2, 288, n_z * 128), BF16),
            pltpu.VMEM((n_x, 2, half, 128), F32),
            pltpu.VMEM((n_x, 136, 128), F32),
            pltpu.VMEM((2 * n_x, 136, 128), F32),
            pltpu.VMEM((136, 128), F32),
            pltpu.VMEM((max(n_gz // 2 - 1, 1), 136, 128), F32),
            pltpu.VMEM((5, half, 128), F32),
            pltpu.VMEM((8, 128), F32),
            pltpu.VMEM((8, 128), F32),
            pltpu.VMEM((8, 128), F32),
            pltpu.VMEM((8, 128), F32),
            pltpu.VMEM((2, width_x, 128), F32),
            pltpu.VMEM((8, 128), F32),
            pltpu.VMEM((8, 128), F32),
            pltpu.VMEM((8, 128), F32),
            pltpu.VMEM((8, 128), F32),
            pltpu.VMEM((2, width_x, 128), F32),
            dma((9,)),
            dma((5,)),
            dma((n_z,)),
            dma((n_z,)),
            dma((n_x,)),
            dma((2 * n_x,)),
            dma((1,)),
            dma((max(n_gz // 2 - 1, 1),)),
            dma((6,)),
            dma((6,)),
            pltpu.SemaphoreType.REGULAR,
            pltpu.SemaphoreType.REGULAR,
        ],
        compiler_params=pltpu.CompilerParams(
            collective_id=0, has_side_effects=True, vmem_limit_bytes=60 * 1024 * 1024
        ),
    )(cot, cosines, wavenumber, time_phase, pole_table, e_field, h_field, pole_current, material)
    return tuple(
        pl.pallas_call(
            put,
            out_shape=(field, field, field),
            in_specs=[vmem] * 3,
            out_specs=(vmem,) * 3,
            compiler_params=pltpu.CompilerParams(vmem_limit_bytes=60 * 1024 * 1024),
        )(*results)
    )


def solution(mesh):
    sizes = (mesh.shape["gx"], PLANES, mesh.shape["gy"] // PLANES, mesh.shape["gz"])
    field = P(None, "gz", "gx", "gy")
    in_specs = (
        field,
        field,
        field,
        P("gz", "gx", "gy"),
        P(),
        P(None, None, ("gx", "gy", "gz")),
        P(None, ("gx", "gy", "gz")),
        P(),
        P(),
    )
    return jax.shard_map(
        functools.partial(local, sizes),
        mesh=mesh,
        in_specs=in_specs,
        out_specs=(field, field, field),
        check_vma=False,
    )
```
